256 devices in a mesh: gx: 16 (over y_hi, z), gy: 16 (over y_lo, x, core).
Axes of the slice: x: 4, y: 4 (y_hi: 2, y_lo: 2; y = y_hi * 2 + y_lo), z: 8, core: 2. Of those that a mesh axis runs over, the one named last changes fastest.
Arguments:
- input_field: bfloat16 [64, 64, 128, 128], P(None, 'gx', 'gy'), may hold values from -6 to 6
- first_weight: bfloat16 [3, 3, 3, 64, 64], replicated, may hold values from -0.15625 to 0.15625
- first_bias: float32 [64], replicated, may hold values from -3 to 3
- down_weight: bfloat16 [2, 2, 2, 128, 64], replicated, may hold values from -0.25 to 0.25
- down_bias: float32 [128], replicated, may hold values from -3 to 3
- second_weight: bfloat16 [3, 3, 3, 128, 128], replicated, may hold values from -0.109375 to 0.109375
- second_bias: float32 [128], replicated, may hold values from -3 to 3
- third_weight: bfloat16 [3, 3, 3, 128, 128], replicated, may hold values from -0.109375 to 0.109375
- third_bias: float32 [128], replicated, may hold values from -3 to 3
- up_weight: bfloat16 [2, 2, 2, 64, 128], replicated, may hold values from -0.5 to 0.5
- up_bias: float32 [64], replicated, may hold values from -3 to 3
- last_weight: bfloat16 [3, 3, 3, 64, 64], replicated, may hold values from -0.15625 to 0.15625
- last_bias: float32 [64], replicated, may hold values from -3 to 3
Outputs:
- output_field: bfloat16 [64, 64, 128, 128], P(None, 'gx', 'gy')
The draws below stay inside these ranges and needn't reach their ends.
All inputs are finite; a program needn't handle non-finite values.
Results may differ from the reference program's by a relative error of at most 0.009.
Values may be sent and summed in bfloat16 or wider, within the bound.
A program may use at most 64 MiB of HBM per device.

```python
import jax
import jax.numpy as jnp

C1 = 64
C2 = 128
NZ = 128
NX = 64
NY = 128


def shard_levels(rng, extent, pieces, low, largest):
    def one(axis_at, shards_of):
        steps = jax.random.uniform(jax.random.fold_in(jax.random.fold_in(rng, 6), axis_at), (shards_of,), jnp.float32, low / len(pieces), largest / len(pieces))
        return jnp.repeat(jnp.exp(steps), extent[axis_at] // shards_of).reshape((-1,) + (1,) * (len(extent) - axis_at - 1))

    factor_of = one(*pieces[0])
    for cut in pieces[1:]:
        factor_of = factor_of * one(*cut)
    return factor_of


def gaussian(key, dims, scale, bound, shards=(), kind=jnp.bfloat16):
    values = jax.random.normal(key, dims, jnp.float32) * scale
    if len(shards) > 0:
        values = shard_levels(key, dims, shards, -0.22, 0.18) * values
    return jnp.clip(values, min=-bound, max=bound).astype(kind)


def setup_inputs(seed: int = 0) -> dict:
    splits = jax.random.split(jax.random.key(seed), 14)
    input_field = gaussian(splits[0], (C1, NX, NY, NZ), 1.0, 6.0, ((1, 16), (2, 16)))
    first_weight = gaussian(splits[1], (3, 3, 3, C1, C1), (27 * C1) ** -0.5, 0.15625)
    first_bias = gaussian(splits[2], (C1,), 0.5, 3.0, (), jnp.float32)
    down_weight = gaussian(splits[3], (2, 2, 2, C2, C1), (8 * C1) ** -0.5, 0.25)
    down_bias = gaussian(splits[4], (C2,), 0.5, 3.0, (), jnp.float32)
    second_weight = gaussian(splits[5], (3, 3, 3, C2, C2), (27 * C2) ** -0.5, 0.109375)
    second_bias = gaussian(splits[6], (C2,), 0.5, 3.0, (), jnp.float32)
    third_weight = gaussian(splits[7], (3, 3, 3, C2, C2), (27 * C2) ** -0.5, 0.109375)
    third_bias = gaussian(splits[8], (C2,), 0.5, 3.0, (), jnp.float32)
    up_weight = gaussian(splits[9], (2, 2, 2, C1, C2), C2 ** -0.5, 0.5)
    up_bias = gaussian(splits[10], (C1,), 0.5, 3.0, (), jnp.float32)
    last_weight = gaussian(splits[11], (3, 3, 3, C1, C1), (27 * C1) ** -0.5, 0.15625)
    last_bias = gaussian(splits[12], (C1,), 0.5, 3.0, (), jnp.float32)
    return {"input_field": input_field, "first_weight": first_weight, "first_bias": first_bias, "down_weight": down_weight, "down_bias": down_bias, "second_weight": second_weight, "second_bias": second_bias, "third_weight": third_weight, "third_bias": third_bias, "up_weight": up_weight, "up_bias": up_bias, "last_weight": last_weight, "last_bias": last_bias}


def leaky_unit(values):
    return jnp.where(values > 0, values, 0.2 * values)


def periodic_conv(field, weight):
    source = field.astype(jnp.float32)
    kernel = weight.astype(jnp.float32)
    summed = jnp.zeros((kernel.shape[3],) + field.shape[1:], jnp.float32)
    for shift_x in range(3):
        for shift_y in range(3):
            for shift_z in range(3):
                moved = jnp.roll(source, (1 - shift_x, 1 - shift_y, 1 - shift_z), axis=(1, 2, 3))
                summed = summed + jnp.einsum("oc,cxyz->oxyz", kernel[shift_x, shift_y, shift_z], moved)
    return summed


def shrink(field, weight):
    chans, wide_x, wide_y, wide_z = field.shape
    blocks = field.astype(jnp.float32).reshape(chans, wide_x // 2, 2, wide_y // 2, 2, wide_z // 2, 2)
    return jnp.einsum("pqroc,cipjqkr->oijk", weight.astype(jnp.float32), blocks)


def expand(field, weight):
    chans, wide_x, wide_y, wide_z = field.shape
    spread = jnp.einsum("pqroc,cijk->oipjqkr", weight.astype(jnp.float32), field.astype(jnp.float32))
    return spread.reshape(weight.shape[3], 2 * wide_x, 2 * wide_y, 2 * wide_z)


def column(bias):
    return bias[:, None, None, None]


def reference(input_field, first_weight, first_bias, down_weight, down_bias, second_weight, second_bias, third_weight, third_bias, up_weight, up_bias, last_weight, last_bias):
    skip = leaky_unit(periodic_conv(input_field, first_weight) + column(first_bias)).astype(jnp.bfloat16)
    coarse = leaky_unit(shrink(skip, down_weight) + column(down_bias)).astype(jnp.bfloat16)
    middle = leaky_unit(periodic_conv(coarse, second_weight) + column(second_bias)).astype(jnp.bfloat16)
    final_coarse = (coarse.astype(jnp.float32) + leaky_unit(periodic_conv(middle, third_weight) + column(third_bias))).astype(jnp.bfloat16)
    merged = (leaky_unit(expand(final_coarse, up_weight) + column(up_bias)) + skip.astype(jnp.float32)).astype(jnp.bfloat16)
    return (periodic_conv(merged, last_weight) + column(last_bias)).astype(jnp.bfloat16)
```

```python
import functools

import jax
import jax.numpy as jnp
from jax import lax
from jax.experimental import pallas as pl
from jax.experimental.pallas import tpu as pltpu
from jax.sharding import PartitionSpec as P

BF16 = jnp.bfloat16
F32 = jnp.float32
MESH = pl.DeviceIdType.MESH

C1 = 64
C2 = 128
NZ = 128
HALF = NZ // 2
FX, FY = 4, 8
CX, CY = 2, 4
WAYS = ((1, 0), (-1, 0), (0, 1), (0, -1), (1, 1), (1, -1), (-1, 1), (-1, -1))
FACES_X = ((1, 0), (-1, 0))
FACES_Y = ((0, 1), (0, -1))
CORNERS = WAYS[4:]
IN, COARSE, SKIP, FINAL = range(4)


def leaky(values):
    return jnp.maximum(values, 0.2 * values)


def nn(a, b):
    return lax.dot_general(a, b, (((1,), (0,)), ((), ())), preferred_element_type=F32)


def nt(a, b):
    return lax.dot_general(a, b, (((1,), (1,)), ((), ())), preferred_element_type=F32)


def lanes(parts):
    return jnp.concatenate(parts, axis=1)


def rows(parts):
    return jnp.concatenate(parts, axis=0)


def span(step, size):
    return {1: (size, 0, 1), -1: (1, size + 1, 1), 0: (1, 1, size)}[step]


def kernel(
    nx,
    ny,
    x_hbm,
    w1_hbm,
    wd_hbm,
    w2_hbm,
    w3_hbm,
    wu_hbm,
    w4_hbm,
    b1_hbm,
    bd_hbm,
    b2_hbm,
    b3_hbm,
    bu_hbm,
    b4_hbm,
    out,
    xin,
    beside,
    flat,
    beside_flat,
    acc,
    fine,
    skip,
    merged,
    coarse,
    middle,
    final,
    w1,
    w4,
    wd,
    w2,
    w3,
    wu,
    big1,
    big4,
    edge1,
    edge4,
    b1,
    bd,
    b2,
    b3,
    bu,
    b4,
    col,
    turned2,
    turned3,
    mine,
    third,
    send_sem,
    recv_sem,
    load_sem,
):
    gx, gy = lax.axis_index("gx"), lax.axis_index("gy")

    def device(way):
        return (lax.rem(gx + way[0] + nx, nx), lax.rem(gy + way[1] + ny, ny))

    late_front = lax.rem(gx, nx // 2) == 0

    def each_side(body):
        for late, order in ((True, (1, 0)), (False, (0, 1))):

            @pl.when(late_front if late else jnp.logical_not(late_front))
            def _():
                for k, side in enumerate(order):
                    body(side, k == 0)

    barrier = pltpu.get_barrier_semaphore()
    for way in WAYS:
        pl.semaphore_signal(barrier, inc=1, device_id=device(way), device_id_type=MESH)

    pairs = (
        (x_hbm, xin),
        (w1_hbm, w1),
        (b1_hbm, b1),
        (w4_hbm, w4),
        (wd_hbm, wd),
        (bd_hbm, bd),
        (w2_hbm, w2),
        (b2_hbm, b2),
        (w3_hbm, w3),
        (b3_hbm, b3),
        (wu_hbm, wu),
        (bu_hbm, bu),
        (b4_hbm, b4),
    )
    loads = [pltpu.make_async_copy(s, d, load_sem.at[k]) for k, (s, d) in enumerate(pairs)]
    for load in loads:
        load.start()
    def loaded(*refs):
        for load, (_, ref) in zip(loads, pairs):
            if any(ref is r for r in refs):
                load.wait()

    loaded(xin)
    pl.semaphore_wait(barrier, len(WAYS))

    face_moves = [
        pltpu.make_async_remote_copy(
            src_ref=xin.at[:, (FX - 1) * (1 - side)],
            dst_ref=beside.at[side],
            send_sem=send_sem.at[IN, side],
            recv_sem=recv_sem.at[IN, side],
            device_id=device(FACES_X[side]),
            device_id_type=MESH,
        )
        for side in range(2)
    ]
    for move in face_moves:
        move.start()

    def piece(buffer, phase, slot, way, xs, ys):
        return pltpu.make_async_remote_copy(
            src_ref=buffer.at[pl.ds(xs[0], xs[2]), pl.ds(ys[0], ys[2])],
            dst_ref=buffer.at[pl.ds(xs[1], xs[2]), pl.ds(ys[1], ys[2])],
            send_sem=send_sem.at[phase, slot],
            recv_sem=recv_sem.at[phase, slot],
            device_id=device(way),
            device_id_type=MESH,
        )

    def copies(buffer, phase, wide, high, chunks):
        made = {}
        for k, way in enumerate(WAYS):
            xs, ys = span(way[0], wide), span(way[1], high)
            if way in FACES_X:
                made[way] = [
                    piece(buffer, phase, 8 + 4 * k + c, way, xs, (1 + first, 1 + first, count))
                    for c, (first, count) in enumerate(chunks)
                ]
            else:
                made[way] = [piece(buffer, phase, k, way, xs, ys)]
        return made

    moves = {
        SKIP: copies(skip, SKIP, FX, FY, [(0, FY // 2), (FY // 2, FY // 2)]),
        FINAL: copies(final, FINAL, CX, CY, [(0, CY)]),
    }
    def double(step, size):
        return {1: (size, 0, 2), -1: (2, size + 2, 2), 0: (2, 2, size)}[step]

    moves[COARSE] = {
        way: [piece(coarse, COARSE, k, way, double(way[0], CX), double(way[1], CY))]
        for k, way in enumerate(WAYS)
    }
    moves[IN] = {
        way: [piece(fine, IN, k, way, span(way[0], FX), span(way[1], FY))]
        for k, way in enumerate(WAYS)
        if k >= 2
    }
    for side in range(2):
        moves[IN][FACES_X[side]] = [face_moves[side]]

    def start(phase, ways=WAYS, chunks=None):
        for way in ways:
            for k, move in enumerate(moves[phase][way]):
                if chunks is None or k in chunks:
                    move.start()

    def arrived(phase, ways):
        for way in ways:
            for move in moves[phase][way]:
                move.wait_recv()

    flat[...] = xin[...].astype(F32).reshape(C1 * FX * FY, NZ)
    columns = [(x, y) for x in range(FX) for y in range(FY)]

    def end(pair):
        return (pair[1] in (0, FY - 1)) + (pair[1] in (0, FY - 1) and pair[0] in (0, FX - 1))

    columns.sort(key=end, reverse=True)
    for k, (x, y) in enumerate(columns):
        tile = flat[pl.ds(x * FY + y, C1, stride=FX * FY), :]
        fine[1 + x, 1 + y] = tile.astype(BF16)
        if k == len(CORNERS) - 1:
            start(IN, CORNERS)
        if k == 2 * FX - 1:
            start(IN, FACES_Y)

    def ways_of(step):
        return [(step, 1), (step, -1), (step, 0)]

    def column(slot, bias):
        square = (C1, C1)
        mask = lax.broadcasted_iota(jnp.int32, square, 0) == lax.broadcasted_iota(
            jnp.int32, square, 1
        )
        kept = jnp.where(mask, jnp.broadcast_to(bias[...], square), 0.0)
        col[slot] = jnp.broadcast_to(jnp.sum(kept, axis=1, keepdims=True), (C1, NZ))

    def arrange(w, big, edge):
        blank = jnp.zeros((C1, C1), BF16)
        for dz in range(3):
            for out_x in range(FX):
                row = (dz * FX + out_x) * C1
                for pair in range(FX * 3 // 2):
                    halves = []
                    for k in (2 * pair, 2 * pair + 1):
                        dx = k // 3 - out_x + 1
                        halves.append(w[dx, k % 3, dz] if 0 <= dx < 3 else blank)
                    big[pl.ds(row, C1), pl.ds(128 * pair, 128)] = lanes(halves)
            for side in range(2):
                row = pl.ds(dz * C1, C1)
                edge[side, row, pl.ds(0, 2 * C1)] = lanes([w[2 * side, 0, dz], w[2 * side, 1, dz]])
                edge[side, row, pl.ds(2 * C1, C1)] = w[2 * side, 2, dz]

    loaded(w1, b1)
    arrange(w1, big1, edge1)
    column(0, b1)

    def turn(part, count):
        return (
            pltpu.roll(part[:count], 1, 1)
            + part[count : 2 * count]
            + pltpu.roll(part[2 * count :], NZ - 1, 1)
        )

    def conv_own(field, big, ys, finish):
        window = [field[pl.ds(1, FX), pl.ds(y, 3)].reshape(FX * 3 * C1, NZ) for y in ys]
        made = nn(big[...], lanes(window))
        for t, y in enumerate(ys):
            total = turn(made[:, NZ * t : NZ * t + NZ], FX * C1)
            for x in range(FX):
                part = total[C1 * x : C1 * (x + 1)]
                if x in (0, FX - 1):
                    acc[y, x // (FX - 1)] = part
                else:
                    finish(x, y, part)

    def conv_edge(field, edge, side, ys, finish):
        window = [field[(FX + 1) * side, pl.ds(y, 3)].reshape(3 * C1, NZ) for y in ys]
        made = nn(edge[side], lanes(window))
        for t, y in enumerate(ys):
            part = acc[y, side] + turn(made[:, NZ * t : NZ * t + NZ], C1)
            finish((FX - 1) * side, y, part)

    def finish_first(x, y, part):
        skip[1 + x, 1 + y] = leaky(part + col[0]).astype(BF16)

    def finish_last(x, y, part):
        flat[pl.ds(x * FY + y, C1, stride=FX * FY), :] = part + col[2]

    def turn_weights(w, turned):
        for dx in range(3):
            for dy in range(3):
                turned[dx, dy] = w[dx, dy].T

    conv_own(fine, big1, (2, 3, 4, 5), finish_first)
    arrived(IN, FACES_Y)
    conv_own(fine, big1, (0, 1, 6, 7), finish_first)

    loaded(wd, bd)
    at_row = lax.broadcasted_iota(jnp.int32, (NZ, NZ), 0)
    at_lane = lax.broadcasted_iota(jnp.int32, (NZ, NZ), 1)
    pick = (at_lane == 2 * lax.rem(at_row, HALF) + at_row // HALF).astype(F32).astype(BF16)
    down = rows([wd[px, py, pz] for pz in range(2) for px in range(2) for py in range(2)])
    def take_side(side, _):
        for move in moves[IN][FACES_X[side]]:
            move.wait_recv()
        beside_flat[side] = beside[side].astype(F32).reshape(C1 * FY, NZ)
        for y in range(FY):
            tile = beside_flat[side, pl.ds(y, C1, stride=FY), :]
            fine[(FX + 1) * side, 1 + y] = tile.astype(BF16)
        arrived(IN, ways_of(1 - 2 * side)[:2])
        conv_edge(fine, edge1, side, range(FY), finish_first)

        split = []
        for j in range(CY):
            block = skip[pl.ds(1 + 2 * side, 2), pl.ds(1 + 2 * j, 2)].reshape(4 * C1, NZ)
            moved = nt(pick, block).astype(BF16)
            split.append(lanes([moved[:HALF], moved[HALF:]]))
        value = leaky(nn(rows(split), down) + bd[...]).astype(BF16)
        coarse[2 + side, pl.ds(2, CY)] = value.reshape(CY, HALF, C2)

    loaded(w2, b2)
    turn_weights(w2, turned2)
    each_side(take_side)
    start(COARSE, CORNERS + FACES_X + FACES_Y)

    def sent(phase):
        for way in WAYS:
            for move in moves[phase][way]:
                move.wait_send()

    def along_z(part):
        return (
            pltpu.roll(part[:, :C2], 1, 0)
            + part[:, C2 : 2 * C2]
            + pltpu.roll(part[:, 2 * C2 :], HALF - 1, 0)
        )

    def taken(field, xs, high):
        return lanes(
            [field[x, pl.ds(dy, high)].reshape(high * HALF, C2) for dy in range(3) for x in xs]
        )

    def weights(turned, xs, outs):
        blank = jnp.zeros((C2, 3 * C2), BF16)
        return rows(
            [
                lanes([turned[x - o + 1, dy] if abs(x - o) <= 1 else blank for o in outs])
                for dy in range(3)
                for x in xs
            ]
        )

    def finish_middle(i, j, part):
        middle[i, j] = leaky(part + b2[...]).astype(BF16)

    def finish_final(i, j, part):
        grown = coarse[2 + i, 2 + j].astype(F32) + leaky(part + b3[...])
        final[1 + i, 1 + j] = grown.astype(BF16)

    def meanwhile():
        start(SKIP, CORNERS)
        start(SKIP, FACES_X)
        start(SKIP, FACES_Y)
        loaded(w3, b3)
        turn_weights(w3, turned3)
        loaded(w4, b4, bu)
        arrange(w4, big4, edge4)
        column(1, bu)
        column(2, b4)

    arrived(COARSE, FACES_Y)
    high = CY + 2
    made = nn(taken(coarse, (2, 3), high), weights(turned2, (2, 3), (2, 3)))
    mine[1] = made[:, : 3 * C2]
    mine[2] = made[:, 3 * C2 :]
    mine[0] = nn(taken(coarse, (2,), high), weights(turned2, (2,), (1,)))
    mine[3] = nn(taken(coarse, (3,), high), weights(turned2, (3,), (4,)))
    meanwhile()

    def ring_side(side, first):
        arrived(COARSE, ways_of(1 - 2 * side))
        xs, outs = ((0, 1), (1, 2)) if side == 0 else ((4, 5), (3, 4))
        made = nn(taken(coarse, xs, high), weights(turned2, xs, outs))
        for k, o in enumerate(outs):
            total = mine[o - 1] + made[:, 3 * C2 * k : 3 * C2 * (k + 1)]
            for j in range(high):
                finish_middle(o - 1, j, along_z(total[j * HALF : (j + 1) * HALF]))
        xs = (2 * side, 2 * side + 1)
        made = nn(taken(middle, xs, CY), weights(turned3, xs, (1, 2)))
        third[...] = made if first else third[...] + made

    each_side(ring_side)
    for i in (1, 0):
        for j in range(CY):
            part = third[pl.ds(j * HALF, HALF), pl.ds(3 * C2 * i, 3 * C2)]
            finish_final(i, j, along_z(part))
        start(FINAL, ways_of(2 * i - 1))
    start(FINAL, FACES_Y)

    loaded(wu)
    at_row = lax.broadcasted_iota(jnp.int32, (2 * HALF, 4 * NZ), 0)
    at_lane = lax.broadcasted_iota(jnp.int32, (2 * HALF, 4 * NZ), 1)
    place = (
        (at_row // HALF == lax.rem(at_lane, 2 * NZ) // NZ)
        & (lax.rem(at_lane, NZ) == 2 * lax.rem(at_row, HALF) + at_lane // (2 * NZ))
    ).astype(F32).astype(BF16)

    def lift(cells, parts):
        wide = []
        for k in range(0, len(cells), 2):
            two = rows([final[i, j] for i, j in cells[k : k + 2]]).T
            spread = nn(two, place).astype(BF16)
            wide.append(rows([spread[:, : 2 * NZ], spread[:, 2 * NZ :]]))
        made = nn(rows([lanes([wu[px, py, 0], wu[px, py, 1]]) for px, py, _ in parts]), lanes(wide))
        for k, (_, _, places) in enumerate(parts):
            for t, spot in enumerate(places):
                if spot is None:
                    continue
                x, y = spot
                value = leaky(made[C1 * k : C1 * (k + 1), NZ * t : NZ * (t + 1)] + col[1])
                merged[x, y] = (value + skip[x, y].astype(F32)).astype(BF16)

    def lift_all(cells, which):
        parts = []
        for px, py in which:
            places = [(2 * i - 1 + px, 2 * j - 1 + py) for i, j in cells]
            parts.append((px, py, [(x, y) if 0 <= y < FY + 2 else None for x, y in places]))
        lift(cells, parts)

    every = [(px, py) for px in range(2) for py in range(2)]
    for i in range(1, 1 + CX):
        lift_all([(i, j) for j in range(1, 1 + CY)], every)
    conv_own(merged, big4, (2, 3, 4, 5), finish_last)
    arrived(SKIP, FACES_Y)
    arrived(FINAL, FACES_Y)
    lift_all([(1, 0), (2, 0)], [(0, 1), (1, 1)])
    lift_all([(1, CY + 1), (2, CY + 1)], [(0, 0), (1, 0)])
    conv_own(merged, big4, (0, 1, 6, 7), finish_last)
    for phase in (IN, COARSE, SKIP):
        sent(phase)
    for side in (1, 0):
        arrived(SKIP, ways_of(1 - 2 * side))
        arrived(FINAL, ways_of(1 - 2 * side))
        i, px = ((0, 1), (CX + 1, 0))[side]
        lift_all([(i, j) for j in range(CY + 2)], [(px, 0), (px, 1)])
        conv_edge(merged, edge4, side, range(FY), finish_last)
    out[...] = flat[...].astype(BF16)
    sent(FINAL)


def body(nx, ny, x, w1, b1, wd, bd, w2, b2, w3, b3, wu, bu, w4, b4):
    count = C1 * FX * FY
    any_space = pl.BlockSpec(memory_space=pl.ANY)
    padded = pltpu.VMEM((FX + 2, FY + 2, C1, NZ), BF16)
    padded_coarse = pltpu.VMEM((CX + 2, CY + 2, HALF, C2), BF16)
    conv = pltpu.VMEM((3, 3, 3, C1, C1), BF16)
    conv_coarse = pltpu.VMEM((3, 3, 3 * C2, C2), BF16)
    turned = pltpu.VMEM((3, 3, C2, 3 * C2), BF16)
    big = pltpu.VMEM((3 * FX * C1, 3 * FX * C1), BF16)
    edge = pltpu.VMEM((2, 3 * C1, 3 * C1), BF16)
    args = (
        x,
        w1,
        jnp.swapaxes(wd, 3, 4),
        w2.reshape(3, 3, 3 * C2, C2),
        w3.reshape(3, 3, 3 * C2, C2),
        wu,
        w4,
        b1.reshape(1, C1),
        bd.reshape(1, C2),
        b2.reshape(1, C2),
        b3.reshape(1, C2),
        bu.reshape(1, C1),
        b4.reshape(1, C1),
    )
    out = pl.pallas_call(
        functools.partial(kernel, nx, ny),
        out_shape=jax.ShapeDtypeStruct((count, NZ), BF16),
        in_specs=[any_space] * 13,
        out_specs=pl.BlockSpec(memory_space=pltpu.VMEM),
        scratch_shapes=[
            pltpu.VMEM((C1, FX, FY, NZ), BF16),
            pltpu.VMEM((2, C1, FY, NZ), BF16),
            pltpu.VMEM((count, NZ), F32),
            pltpu.VMEM((2, C1 * FY, NZ), F32),
            pltpu.VMEM((FY, 2, C1, NZ), F32),
            padded,
            padded,
            padded,
            pltpu.VMEM((CX + 4, CY + 4, HALF, C2), BF16),
            padded_coarse,
            padded_coarse,
            conv,
            conv,
            pltpu.VMEM((2, 2, 2, C1, C2), BF16),
            conv_coarse,
            conv_coarse,
            pltpu.VMEM((2, 2, 2, C1, C2), BF16),
            big,
            big,
            edge,
            edge,
            pltpu.VMEM((1, C1), F32),
            pltpu.VMEM((1, C2), F32),
            pltpu.VMEM((1, C2), F32),
            pltpu.VMEM((1, C2), F32),
            pltpu.VMEM((1, C1), F32),
            pltpu.VMEM((1, C1), F32),
            pltpu.VMEM((3, C1, NZ), F32),
            turned,
            turned,
            pltpu.VMEM((CX + 2, (CY + 2) * HALF, 3 * C2), F32),
            pltpu.VMEM((CY * HALF, CX * 3 * C2), F32),
            pltpu.SemaphoreType.DMA((4, 16)),
            pltpu.SemaphoreType.DMA((4, 16)),
            pltpu.SemaphoreType.DMA((13,)),
        ],
        compiler_params=pltpu.CompilerParams(
            collective_id=0, has_side_effects=True, vmem_limit_bytes=48 * 1024 * 1024
        ),
    )(*(pltpu.with_memory_space_constraint(arg, pltpu.HBM) for arg in args))
    return out.reshape(C1, FX, FY, NZ)


def solution(mesh):
    sharded = P(None, "gx", "gy", None)
    return jax.shard_map(
        functools.partial(body, mesh.shape["gx"], mesh.shape["gy"]),
        mesh=mesh,
        in_specs=(sharded,) + (P(),) * 12,
        out_specs=sharded,
        check_vma=False,
    )
```

```python
import functools

import jax
import jax.numpy as jnp
from jax import lax
from jax.experimental import pallas as pl
from jax.experimental.pallas import tpu as pltpu
from jax.sharding import PartitionSpec as P

BF16 = jnp.bfloat16
F32 = jnp.float32
MESH = pl.DeviceIdType.MESH

C1 = 64
C2 = 128
NZ = 128
HALF = NZ // 2
FX, FY = 4, 8
CX, CY = 2, 4
WAYS = ((1, 0), (-1, 0), (0, 1), (0, -1), (1, 1), (1, -1), (-1, 1), (-1, -1))
FACES_X = ((1, 0), (-1, 0))
FACES_Y = ((0, 1), (0, -1))
CORNERS = WAYS[4:]
IN, COARSE, SKIP, FINAL = range(4)


def leaky(values):
    return jnp.maximum(values, 0.2 * values)


def nn(a, b):
    return lax.dot_general(a, b, (((1,), (0,)), ((), ())), preferred_element_type=F32)


def nt(a, b):
    return lax.dot_general(a, b, (((1,), (1,)), ((), ())), preferred_element_type=F32)


def lanes(parts):
    return jnp.concatenate(parts, axis=1)


def rows(parts):
    return jnp.concatenate(parts, axis=0)


def span(step, size):
    return {1: (size, 0, 1), -1: (1, size + 1, 1), 0: (1, 1, size)}[step]


def kernel(
    nx,
    ny,
    x_hbm,
    w1_hbm,
    wd_hbm,
    w2_hbm,
    w3_hbm,
    wu_hbm,
    w4_hbm,
    b1_hbm,
    bd_hbm,
    b2_hbm,
    b3_hbm,
    bu_hbm,
    b4_hbm,
    out,
    xin,
    beside,
    flat,
    beside_flat,
    acc,
    fine,
    skip,
    merged,
    coarse,
    middle,
    final,
    w1,
    w4,
    wd,
    w2,
    w3,
    wu,
    big1,
    big4,
    edge1,
    edge4,
    b1,
    bd,
    b2,
    b3,
    bu,
    b4,
    col,
    turned2,
    turned3,
    mine,
    third,
    send_sem,
    recv_sem,
    load_sem,
):
    gx, gy = lax.axis_index("gx"), lax.axis_index("gy")

    def device(way):
        return (lax.rem(gx + way[0] + nx, nx), lax.rem(gy + way[1] + ny, ny))

    late_front = lax.rem(gx, nx // 2) == 0

    def each_side(body):
        for late, order in ((True, (1, 0)), (False, (0, 1))):

            @pl.when(late_front if late else jnp.logical_not(late_front))
            def _():
                for k, side in enumerate(order):
                    body(side, k == 0)

    barrier = pltpu.get_barrier_semaphore()
    for way in WAYS:
        pl.semaphore_signal(barrier, inc=1, device_id=device(way), device_id_type=MESH)

    pairs = (
        (x_hbm, xin),
        (w1_hbm, w1),
        (b1_hbm, b1),
        (w4_hbm, w4),
        (wd_hbm, wd),
        (bd_hbm, bd),
        (w2_hbm, w2),
        (b2_hbm, b2),
        (w3_hbm, w3),
        (b3_hbm, b3),
        (wu_hbm, wu),
        (bu_hbm, bu),
        (b4_hbm, b4),
    )
    loads = [pltpu.make_async_copy(s, d, load_sem.at[k]) for k, (s, d) in enumerate(pairs)]
    for load in loads:
        load.start()
    def loaded(*refs):
        for load, (_, ref) in zip(loads, pairs):
            if any(ref is r for r in refs):
                load.wait()

    loaded(xin)
    pl.semaphore_wait(barrier, len(WAYS))

    face_moves = [
        pltpu.make_async_remote_copy(
            src_ref=xin.at[:, (FX - 1) * (1 - side)],
            dst_ref=beside.at[side],
            send_sem=send_sem.at[IN, side],
            recv_sem=recv_sem.at[IN, side],
            device_id=device(FACES_X[side]),
            device_id_type=MESH,
        )
        for side in range(2)
    ]
    for move in face_moves:
        move.start()

    def piece(buffer, phase, slot, way, xs, ys):
        return pltpu.make_async_remote_copy(
            src_ref=buffer.at[pl.ds(xs[0], xs[2]), pl.ds(ys[0], ys[2])],
            dst_ref=buffer.at[pl.ds(xs[1], xs[2]), pl.ds(ys[1], ys[2])],
            send_sem=send_sem.at[phase, slot],
            recv_sem=recv_sem.at[phase, slot],
            device_id=device(way),
            device_id_type=MESH,
        )

    def copies(buffer, phase, wide, high, chunks):
        made = {}
        for k, way in enumerate(WAYS):
            xs, ys = span(way[0], wide), span(way[1], high)
            if way in FACES_X:
                made[way] = [
                    piece(buffer, phase, 8 + 4 * k + c, way, xs, (1 + first, 1 + first, count))
                    for c, (first, count) in enumerate(chunks)
                ]
            else:
                made[way] = [piece(buffer, phase, k, way, xs, ys)]
        return made

    moves = {
        SKIP: copies(skip, SKIP, FX, FY, [(0, FY // 2), (FY // 2, FY // 2)]),
        FINAL: copies(final, FINAL, CX, CY, [(0, CY)]),
    }
    column_x = {1: 0, -1: CX + 2, 0: 2}
    double_y = {1: (CY, 0, 2), -1: (2, CY + 2, 2), 0: (2, 2, CY)}
    moves[COARSE] = {
        way: [
            piece(coarse, COARSE, 2 * k + i, way, (2 + i, column_x[way[0]] + i, 1), double_y[way[1]])
            for i in range(CX)
        ]
        for k, way in enumerate(WAYS)
    }
    moves[IN] = {
        way: [piece(fine, IN, k, way, span(way[0], FX), span(way[1], FY))]
        for k, way in enumerate(WAYS)
        if k >= 2
    }
    for side in range(2):
        moves[IN][FACES_X[side]] = [face_moves[side]]

    def start(phase, ways=WAYS, chunks=None):
        for way in ways:
            for k, move in enumerate(moves[phase][way]):
                if chunks is None or k in chunks:
                    move.start()

    def arrived(phase, ways):
        for way in ways:
            for move in moves[phase][way]:
                move.wait_recv()

    flat[...] = xin[...].astype(F32).reshape(C1 * FX * FY, NZ)
    columns = [(x, y) for x in range(FX) for y in range(FY)]

    def end(pair):
        return (pair[1] in (0, FY - 1)) + (pair[1] in (0, FY - 1) and pair[0] in (0, FX - 1))

    columns.sort(key=end, reverse=True)
    for k, (x, y) in enumerate(columns):
        tile = flat[pl.ds(x * FY + y, C1, stride=FX * FY), :]
        fine[1 + x, 1 + y] = tile.astype(BF16)
        if k == len(CORNERS) - 1:
            start(IN, CORNERS)
        if k == 2 * FX - 1:
            start(IN, FACES_Y)

    def ways_of(step):
        return [(step, 1), (step, -1), (step, 0)]

    def column(slot, bias):
        square = (C1, C1)
        mask = lax.broadcasted_iota(jnp.int32, square, 0) == lax.broadcasted_iota(
            jnp.int32, square, 1
        )
        kept = jnp.where(mask, jnp.broadcast_to(bias[...], square), 0.0)
        col[slot] = jnp.broadcast_to(jnp.sum(kept, axis=1, keepdims=True), (C1, NZ))

    def arrange(w, big, edge):
        blank = jnp.zeros((C1, C1), BF16)
        for dz in range(3):
            for out_x in range(FX):
                row = (dz * FX + out_x) * C1
                for pair in range(FX * 3 // 2):
                    halves = []
                    for k in (2 * pair, 2 * pair + 1):
                        dx = k // 3 - out_x + 1
                        halves.append(w[dx, k % 3, dz] if 0 <= dx < 3 else blank)
                    big[pl.ds(row, C1), pl.ds(128 * pair, 128)] = lanes(halves)
            for side in range(2):
                row = pl.ds(dz * C1, C1)
                edge[side, row, pl.ds(0, 2 * C1)] = lanes([w[2 * side, 0, dz], w[2 * side, 1, dz]])
                edge[side, row, pl.ds(2 * C1, C1)] = w[2 * side, 2, dz]

    loaded(w1, b1)
    arrange(w1, big1, edge1)
    column(0, b1)

    def turn(part, count):
        return (
            pltpu.roll(part[:count], 1, 1)
            + part[count : 2 * count]
            + pltpu.roll(part[2 * count :], NZ - 1, 1)
        )

    def conv_own(field, big, ys, finish):
        window = [field[pl.ds(1, FX), pl.ds(y, 3)].reshape(FX * 3 * C1, NZ) for y in ys]
        made = nn(big[...], lanes(window))
        for t, y in enumerate(ys):
            total = turn(made[:, NZ * t : NZ * t + NZ], FX * C1)
            for x in range(FX):
                part = total[C1 * x : C1 * (x + 1)]
                if x in (0, FX - 1):
                    acc[y, x // (FX - 1)] = part
                else:
                    finish(x, y, part)

    def conv_edge(field, edge, side, ys, finish):
        window = [field[(FX + 1) * side, pl.ds(y, 3)].reshape(3 * C1, NZ) for y in ys]
        made = nn(edge[side], lanes(window))
        for t, y in enumerate(ys):
            part = acc[y, side] + turn(made[:, NZ * t : NZ * t + NZ], C1)
            finish((FX - 1) * side, y, part)

    def finish_first(x, y, part):
        skip[1 + x, 1 + y] = leaky(part + col[0]).astype(BF16)

    def finish_last(x, y, part):
        flat[pl.ds(x * FY + y, C1, stride=FX * FY), :] = part + col[2]

    def turn_weights(w, turned):
        for dx in range(3):
            for dy in range(3):
                turned[dx, dy] = w[dx, dy].T

    conv_own(fine, big1, (2, 3, 4, 5), finish_first)
    arrived(IN, FACES_Y)
    conv_own(fine, big1, (0, 1, 6, 7), finish_first)

    loaded(wd, bd)
    at_row = lax.broadcasted_iota(jnp.int32, (NZ, NZ), 0)
    at_lane = lax.broadcasted_iota(jnp.int32, (NZ, NZ), 1)
    pick = (at_lane == 2 * lax.rem(at_row, HALF) + at_row // HALF).astype(F32).astype(BF16)
    down = rows([wd[px, py, pz] for pz in range(2) for px in range(2) for py in range(2)])
    def take_side(side, _):
        for move in moves[IN][FACES_X[side]]:
            move.wait_recv()
        beside_flat[side] = beside[side].astype(F32).reshape(C1 * FY, NZ)
        for y in range(FY):
            tile = beside_flat[side, pl.ds(y, C1, stride=FY), :]
            fine[(FX + 1) * side, 1 + y] = tile.astype(BF16)
        arrived(IN, ways_of(1 - 2 * side)[:2])
        conv_edge(fine, edge1, side, range(FY), finish_first)

        split = []
        for j in range(CY):
            block = skip[pl.ds(1 + 2 * side, 2), pl.ds(1 + 2 * j, 2)].reshape(4 * C1, NZ)
            moved = nt(pick, block).astype(BF16)
            split.append(lanes([moved[:HALF], moved[HALF:]]))
        value = leaky(nn(rows(split), down) + bd[...]).astype(BF16)
        coarse[2 + side, pl.ds(2, CY)] = value.reshape(CY, HALF, C2)
        start(COARSE, CORNERS + FACES_X + FACES_Y, (side,))

    loaded(w2, b2)
    turn_weights(w2, turned2)
    each_side(take_side)

    def sent(phase):
        for way in WAYS:
            for move in moves[phase][way]:
                move.wait_send()

    def along_z(part):
        return (
            pltpu.roll(part[:, :C2], 1, 0)
            + part[:, C2 : 2 * C2]
            + pltpu.roll(part[:, 2 * C2 :], HALF - 1, 0)
        )

    def taken(field, xs, high):
        return lanes(
            [field[x, pl.ds(dy, high)].reshape(high * HALF, C2) for dy in range(3) for x in xs]
        )

    def weights(turned, xs, outs):
        blank = jnp.zeros((C2, 3 * C2), BF16)
        return rows(
            [
                lanes([turned[x - o + 1, dy] if abs(x - o) <= 1 else blank for o in outs])
                for dy in range(3)
                for x in xs
            ]
        )

    def finish_middle(i, j, part):
        middle[i, j] = leaky(part + b2[...]).astype(BF16)

    def finish_final(i, j, part):
        grown = coarse[2 + i, 2 + j].astype(F32) + leaky(part + b3[...])
        final[1 + i, 1 + j] = grown.astype(BF16)

    def meanwhile():
        start(SKIP, CORNERS)
        start(SKIP, FACES_X)
        start(SKIP, FACES_Y)
        loaded(w3, b3)
        turn_weights(w3, turned3)
        loaded(w4, b4, bu)
        arrange(w4, big4, edge4)
        column(1, bu)
        column(2, b4)

    arrived(COARSE, FACES_Y)
    high = CY + 2
    made = nn(taken(coarse, (2, 3), high), weights(turned2, (2, 3), (2, 3)))
    mine[1] = made[:, : 3 * C2]
    mine[2] = made[:, 3 * C2 :]
    mine[0] = nn(taken(coarse, (2,), high), weights(turned2, (2,), (1,)))
    mine[3] = nn(taken(coarse, (3,), high), weights(turned2, (3,), (4,)))
    meanwhile()

    def ring_side(side, first):
        arrived(COARSE, ways_of(1 - 2 * side))
        xs, outs = ((0, 1), (1, 2)) if side == 0 else ((4, 5), (3, 4))
        made = nn(taken(coarse, xs, high), weights(turned2, xs, outs))
        for k, o in enumerate(outs):
            total = mine[o - 1] + made[:, 3 * C2 * k : 3 * C2 * (k + 1)]
            for j in range(high):
                finish_middle(o - 1, j, along_z(total[j * HALF : (j + 1) * HALF]))
        if first:
            xs = (2 * side, 2 * side + 1)
            third[...] = nn(taken(middle, xs, CY), weights(turned3, xs, (1, 2)))
            return
        for i in (side, 1 - side):
            xs = (2 * side, 2 * side + 1) if i == side else (1 + side,)
            made = nn(taken(middle, xs, CY), weights(turned3, xs, (1 + i,)))
            total = third[:, pl.ds(3 * C2 * i, 3 * C2)] + made
            for j in range(CY):
                finish_final(i, j, along_z(total[j * HALF : (j + 1) * HALF]))
            start(FINAL, ways_of(2 * i - 1))

    each_side(ring_side)
    start(FINAL, FACES_Y)

    loaded(wu)
    at_row = lax.broadcasted_iota(jnp.int32, (2 * HALF, 4 * NZ), 0)
    at_lane = lax.broadcasted_iota(jnp.int32, (2 * HALF, 4 * NZ), 1)
    place = (
        (at_row // HALF == lax.rem(at_lane, 2 * NZ) // NZ)
        & (lax.rem(at_lane, NZ) == 2 * lax.rem(at_row, HALF) + at_lane // (2 * NZ))
    ).astype(F32).astype(BF16)

    def lift(cells, parts):
        wide = []
        for k in range(0, len(cells), 2):
            two = rows([final[i, j] for i, j in cells[k : k + 2]]).T
            spread = nn(two, place).astype(BF16)
            wide.append(rows([spread[:, : 2 * NZ], spread[:, 2 * NZ :]]))
        made = nn(rows([lanes([wu[px, py, 0], wu[px, py, 1]]) for px, py, _ in parts]), lanes(wide))
        for k, (_, _, places) in enumerate(parts):
            for t, spot in enumerate(places):
                if spot is None:
                    continue
                x, y = spot
                value = leaky(made[C1 * k : C1 * (k + 1), NZ * t : NZ * (t + 1)] + col[1])
                merged[x, y] = (value + skip[x, y].astype(F32)).astype(BF16)

    def lift_all(cells, which):
        parts = []
        for px, py in which:
            places = [(2 * i - 1 + px, 2 * j - 1 + py) for i, j in cells]
            parts.append((px, py, [(x, y) if 0 <= y < FY + 2 else None for x, y in places]))
        lift(cells, parts)

    every = [(px, py) for px in range(2) for py in range(2)]
    for i in range(1, 1 + CX):
        lift_all([(i, j) for j in range(1, 1 + CY)], every)
    conv_own(merged, big4, (2, 3, 4, 5), finish_last)
    arrived(SKIP, FACES_Y)
    arrived(FINAL, FACES_Y)
    lift_all([(1, 0), (2, 0)], [(0, 1), (1, 1)])
    lift_all([(1, CY + 1), (2, CY + 1)], [(0, 0), (1, 0)])
    conv_own(merged, big4, (0, 1, 6, 7), finish_last)
    for phase in (IN, COARSE, SKIP):
        sent(phase)
    for side in (1, 0):
        arrived(SKIP, ways_of(1 - 2 * side))
        arrived(FINAL, ways_of(1 - 2 * side))
        i, px = ((0, 1), (CX + 1, 0))[side]
        lift_all([(i, j) for j in range(CY + 2)], [(px, 0), (px, 1)])
        conv_edge(merged, edge4, side, range(FY), finish_last)
    out[...] = flat[...].astype(BF16)
    sent(FINAL)


def body(nx, ny, x, w1, b1, wd, bd, w2, b2, w3, b3, wu, bu, w4, b4):
    count = C1 * FX * FY
    any_space = pl.BlockSpec(memory_space=pl.ANY)
    padded = pltpu.VMEM((FX + 2, FY + 2, C1, NZ), BF16)
    padded_coarse = pltpu.VMEM((CX + 2, CY + 2, HALF, C2), BF16)
    conv = pltpu.VMEM((3, 3, 3, C1, C1), BF16)
    conv_coarse = pltpu.VMEM((3, 3, 3 * C2, C2), BF16)
    turned = pltpu.VMEM((3, 3, C2, 3 * C2), BF16)
    big = pltpu.VMEM((3 * FX * C1, 3 * FX * C1), BF16)
    edge = pltpu.VMEM((2, 3 * C1, 3 * C1), BF16)
    args = (
        x,
        w1,
        jnp.swapaxes(wd, 3, 4),
        w2.reshape(3, 3, 3 * C2, C2),
        w3.reshape(3, 3, 3 * C2, C2),
        wu,
        w4,
        b1.reshape(1, C1),
        bd.reshape(1, C2),
        b2.reshape(1, C2),
        b3.reshape(1, C2),
        bu.reshape(1, C1),
        b4.reshape(1, C1),
    )
    out = pl.pallas_call(
        functools.partial(kernel, nx, ny),
        out_shape=jax.ShapeDtypeStruct((count, NZ), BF16),
        in_specs=[any_space] * 13,
        out_specs=pl.BlockSpec(memory_space=pltpu.VMEM),
        scratch_shapes=[
            pltpu.VMEM((C1, FX, FY, NZ), BF16),
            pltpu.VMEM((2, C1, FY, NZ), BF16),
            pltpu.VMEM((count, NZ), F32),
            pltpu.VMEM((2, C1 * FY, NZ), F32),
            pltpu.VMEM((FY, 2, C1, NZ), F32),
            padded,
            padded,
            padded,
            pltpu.VMEM((CX + 4, CY + 4, HALF, C2), BF16),
            padded_coarse,
            padded_coarse,
            conv,
            conv,
            pltpu.VMEM((2, 2, 2, C1, C2), BF16),
            conv_coarse,
            conv_coarse,
            pltpu.VMEM((2, 2, 2, C1, C2), BF16),
            big,
            big,
            edge,
            edge,
            pltpu.VMEM((1, C1), F32),
            pltpu.VMEM((1, C2), F32),
            pltpu.VMEM((1, C2), F32),
            pltpu.VMEM((1, C2), F32),
            pltpu.VMEM((1, C1), F32),
            pltpu.VMEM((1, C1), F32),
            pltpu.VMEM((3, C1, NZ), F32),
            turned,
            turned,
            pltpu.VMEM((CX + 2, (CY + 2) * HALF, 3 * C2), F32),
            pltpu.VMEM((CY * HALF, CX * 3 * C2), F32),
            pltpu.SemaphoreType.DMA((4, 16)),
            pltpu.SemaphoreType.DMA((4, 16)),
            pltpu.SemaphoreType.DMA((13,)),
        ],
        compiler_params=pltpu.CompilerParams(
            collective_id=0, has_side_effects=True, vmem_limit_bytes=48 * 1024 * 1024
        ),
    )(*(pltpu.with_memory_space_constraint(arg, pltpu.HBM) for arg in args))
    return out.reshape(C1, FX, FY, NZ)


def solution(mesh):
    sharded = P(None, "gx", "gy", None)
    return jax.shard_map(
        functools.partial(body, mesh.shape["gx"], mesh.shape["gy"]),
        mesh=mesh,
        in_specs=(sharded,) + (P(),) * 12,
        out_specs=sharded,
        check_vma=False,
    )
```

```python
import functools

import jax
import jax.numpy as jnp
from jax import lax
from jax.experimental import pallas as pl
from jax.experimental.pallas import tpu as pltpu
from jax.sharding import PartitionSpec as P

BF16 = jnp.bfloat16
F32 = jnp.float32
MESH = pl.DeviceIdType.MESH

C1 = 64
C2 = 128
NZ = 128
HALF = NZ // 2
FX, FY = 4, 8
CX, CY = 2, 4
WAYS = ((1, 0), (-1, 0), (0, 1), (0, -1), (1, 1), (1, -1), (-1, 1), (-1, -1))
FACES_X = ((1, 0), (-1, 0))
FACES_Y = ((0, 1), (0, -1))
CORNERS = WAYS[4:]
IN, COARSE, SKIP, FINAL = range(4)


def leaky(values):
    return jnp.maximum(values, 0.2 * values)


def nn(a, b):
    return lax.dot_general(a, b, (((1,), (0,)), ((), ())), preferred_element_type=F32)


def nt(a, b):
    return lax.dot_general(a, b, (((1,), (1,)), ((), ())), preferred_element_type=F32)


def lanes(parts):
    return jnp.concatenate(parts, axis=1)


def rows(parts):
    return jnp.concatenate(parts, axis=0)


def span(step, size):
    return {1: (size, 0, 1), -1: (1, size + 1, 1), 0: (1, 1, size)}[step]


def kernel(
    nx,
    ny,
    x_hbm,
    w1_hbm,
    wd_hbm,
    w2_hbm,
    w3_hbm,
    wu_hbm,
    w4_hbm,
    b1_hbm,
    bd_hbm,
    b2_hbm,
    b3_hbm,
    bu_hbm,
    b4_hbm,
    out,
    xin,
    beside,
    flat,
    beside_flat,
    acc,
    fine,
    skip,
    merged,
    coarse,
    middle,
    final,
    w1,
    w4,
    wd,
    w2,
    w3,
    wu,
    big1,
    big4,
    edge1,
    edge4,
    b1,
    bd,
    b2,
    b3,
    bu,
    b4,
    col,
    turned2,
    turned3,
    mine,
    third,
    send_sem,
    recv_sem,
    load_sem,
):
    gx, gy = lax.axis_index("gx"), lax.axis_index("gy")

    def device(way):
        return (lax.rem(gx + way[0] + nx, nx), lax.rem(gy + way[1] + ny, ny))

    late_front = lax.rem(gx, nx // 2) == 0

    def each_side(body):
        for late, order in ((True, (1, 0)), (False, (0, 1))):

            @pl.when(late_front if late else jnp.logical_not(late_front))
            def _():
                for k, side in enumerate(order):
                    body(side, k == 0)

    barrier = pltpu.get_barrier_semaphore()
    for way in WAYS:
        pl.semaphore_signal(barrier, inc=1, device_id=device(way), device_id_type=MESH)

    pairs = (
        (x_hbm, xin),
        (w1_hbm, w1),
        (b1_hbm, b1),
        (w4_hbm, w4),
        (wd_hbm, wd),
        (bd_hbm, bd),
        (w2_hbm, w2),
        (b2_hbm, b2),
        (w3_hbm, w3),
        (b3_hbm, b3),
        (wu_hbm, wu),
        (bu_hbm, bu),
        (b4_hbm, b4),
    )
    loads = [pltpu.make_async_copy(s, d, load_sem.at[k]) for k, (s, d) in enumerate(pairs)]
    for load in loads:
        load.start()
    def loaded(*refs):
        for load, (_, ref) in zip(loads, pairs):
            if any(ref is r for r in refs):
                load.wait()

    loaded(xin)
    columns = [(x, y) for x in range(FX) for y in range(FY)]
    columns.sort(key=lambda pair: pair[1] not in (0, FY - 1))

    def turn_input(some):
        for x, y in some:
            tile = flat[pl.ds(x * FY + y, C1, stride=FX * FY), :]
            fine[1 + x, 1 + y] = tile.astype(BF16)

    flat[...] = xin[...].astype(F32).reshape(C1 * FX * FY, NZ)
    turn_input(columns[: 2 * FX])
    pl.semaphore_wait(barrier, len(WAYS))

    face_moves = [
        pltpu.make_async_remote_copy(
            src_ref=xin.at[:, (FX - 1) * (1 - side)],
            dst_ref=beside.at[side],
            send_sem=send_sem.at[IN, side],
            recv_sem=recv_sem.at[IN, side],
            device_id=device(FACES_X[side]),
            device_id_type=MESH,
        )
        for side in range(2)
    ]
    for move in face_moves:
        move.start()

    def piece(buffer, phase, slot, way, xs, ys):
        return pltpu.make_async_remote_copy(
            src_ref=buffer.at[pl.ds(xs[0], xs[2]), pl.ds(ys[0], ys[2])],
            dst_ref=buffer.at[pl.ds(xs[1], xs[2]), pl.ds(ys[1], ys[2])],
            send_sem=send_sem.at[phase, slot],
            recv_sem=recv_sem.at[phase, slot],
            device_id=device(way),
            device_id_type=MESH,
        )

    def copies(buffer, phase, wide, high, chunks):
        made = {}
        for k, way in enumerate(WAYS):
            xs, ys = span(way[0], wide), span(way[1], high)
            if way in FACES_X:
                made[way] = [
                    piece(buffer, phase, 8 + 4 * k + c, way, xs, (1 + first, 1 + first, count))
                    for c, (first, count) in enumerate(chunks)
                ]
            else:
                made[way] = [piece(buffer, phase, k, way, xs, ys)]
        return made

    moves = {
        SKIP: copies(skip, SKIP, FX, FY, [(0, FY // 2), (FY // 2, FY // 2)]),
        FINAL: copies(final, FINAL, CX, CY, [(0, CY)]),
    }
    column_x = {1: 0, -1: CX + 2, 0: 2}
    double_y = {1: (CY, 0, 2), -1: (2, CY + 2, 2), 0: (2, 2, CY)}
    moves[COARSE] = {
        way: [
            piece(coarse, COARSE, 2 * k + i, way, (2 + i, column_x[way[0]] + i, 1), double_y[way[1]])
            for i in range(CX)
        ]
        for k, way in enumerate(WAYS)
    }
    moves[IN] = {
        way: [piece(fine, IN, k, way, span(way[0], FX), span(way[1], FY))]
        for k, way in enumerate(WAYS)
        if k >= 2
    }
    for side in range(2):
        moves[IN][FACES_X[side]] = [face_moves[side]]

    def start(phase, ways=WAYS, chunks=None):
        for way in ways:
            for k, move in enumerate(moves[phase][way]):
                if chunks is None or k in chunks:
                    move.start()

    def arrived(phase, ways, chunks=None):
        for way in ways:
            for k, move in enumerate(moves[phase][way]):
                if chunks is None or k in chunks:
                    move.wait_recv()

    start(IN, CORNERS + FACES_Y)
    turn_input(columns[2 * FX :])

    def ways_of(step):
        return [(step, 1), (step, -1), (step, 0)]

    def column(slot, bias):
        square = (C1, C1)
        mask = lax.broadcasted_iota(jnp.int32, square, 0) == lax.broadcasted_iota(
            jnp.int32, square, 1
        )
        kept = jnp.where(mask, jnp.broadcast_to(bias[...], square), 0.0)
        col[slot] = jnp.broadcast_to(jnp.sum(kept, axis=1, keepdims=True), (C1, NZ))

    def arrange(w, big, edge):
        blank = jnp.zeros((C1, C1), BF16)
        for dz in range(3):
            for out_x in range(FX):
                row = (dz * FX + out_x) * C1
                for pair in range(FX * 3 // 2):
                    halves = []
                    for k in (2 * pair, 2 * pair + 1):
                        dx = k // 3 - out_x + 1
                        halves.append(w[dx, k % 3, dz] if 0 <= dx < 3 else blank)
                    big[pl.ds(row, C1), pl.ds(128 * pair, 128)] = lanes(halves)
            for side in range(2):
                row = pl.ds(dz * C1, C1)
                edge[side, row, pl.ds(0, 2 * C1)] = lanes([w[2 * side, 0, dz], w[2 * side, 1, dz]])
                edge[side, row, pl.ds(2 * C1, C1)] = w[2 * side, 2, dz]

    loaded(w1, b1)
    arrange(w1, big1, edge1)
    column(0, b1)

    def turn(part, count):
        return (
            pltpu.roll(part[:count], 1, 1)
            + part[count : 2 * count]
            + pltpu.roll(part[2 * count :], NZ - 1, 1)
        )

    def conv_own(field, big, ys, finish):
        window = [field[pl.ds(1, FX), pl.ds(y, 3)].reshape(FX * 3 * C1, NZ) for y in ys]
        made = nn(big[...], lanes(window))
        for t, y in enumerate(ys):
            total = turn(made[:, NZ * t : NZ * t + NZ], FX * C1)
            for x in range(FX):
                part = total[C1 * x : C1 * (x + 1)]
                if x in (0, FX - 1):
                    acc[y, x // (FX - 1)] = part
                else:
                    finish(x, y, part)

    def conv_edge(field, edge, side, ys, finish):
        window = [field[(FX + 1) * side, pl.ds(y, 3)].reshape(3 * C1, NZ) for y in ys]
        made = nn(edge[side], lanes(window))
        for t, y in enumerate(ys):
            part = acc[y, side] + turn(made[:, NZ * t : NZ * t + NZ], C1)
            finish((FX - 1) * side, y, part)

    def finish_first(x, y, part):
        skip[1 + x, 1 + y] = leaky(part + col[0]).astype(BF16)

    def finish_last(x, y, part):
        flat[pl.ds(x * FY + y, C1, stride=FX * FY), :] = part + col[2]

    def turn_weights(w, turned):
        for dx in range(3):
            for dy in range(3):
                turned[dx, dy] = w[dx, dy].T

    conv_own(fine, big1, (2, 3, 4, 5), finish_first)
    arrived(IN, FACES_Y)
    conv_own(fine, big1, (0, 1, 6, 7), finish_first)

    loaded(wd, bd)
    at_row = lax.broadcasted_iota(jnp.int32, (NZ, NZ), 0)
    at_lane = lax.broadcasted_iota(jnp.int32, (NZ, NZ), 1)
    pick = (at_lane == 2 * lax.rem(at_row, HALF) + at_row // HALF).astype(F32).astype(BF16)
    down = rows([wd[px, py, pz] for pz in range(2) for px in range(2) for py in range(2)])
    def take_side(side, _):
        for move in moves[IN][FACES_X[side]]:
            move.wait_recv()
        beside_flat[side] = beside[side].astype(F32).reshape(C1 * FY, NZ)
        for y in range(FY):
            tile = beside_flat[side, pl.ds(y, C1, stride=FY), :]
            fine[(FX + 1) * side, 1 + y] = tile.astype(BF16)
        arrived(IN, ways_of(1 - 2 * side)[:2])
        conv_edge(fine, edge1, side, range(FY), finish_first)

        split = []
        for j in range(CY):
            block = skip[pl.ds(1 + 2 * side, 2), pl.ds(1 + 2 * j, 2)].reshape(4 * C1, NZ)
            moved = nt(pick, block).astype(BF16)
            split.append(lanes([moved[:HALF], moved[HALF:]]))
        value = leaky(nn(rows(split), down) + bd[...]).astype(BF16)
        coarse[2 + side, pl.ds(2, CY)] = value.reshape(CY, HALF, C2)
        start(COARSE, ways_of(2 * side - 1) + ways_of(1 - 2 * side), (side,))
        start(COARSE, FACES_Y, (side,))

    loaded(w2, b2)
    turn_weights(w2, turned2)
    each_side(take_side)

    def sent(phase):
        for way in WAYS:
            for move in moves[phase][way]:
                move.wait_send()

    def along_z(part):
        return (
            pltpu.roll(part[:, :C2], 1, 0)
            + part[:, C2 : 2 * C2]
            + pltpu.roll(part[:, 2 * C2 :], HALF - 1, 0)
        )

    def taken(field, xs, high):
        return lanes(
            [field[x, pl.ds(dy, high)].reshape(high * HALF, C2) for dy in range(3) for x in xs]
        )

    def weights(turned, xs, outs):
        blank = jnp.zeros((C2, 3 * C2), BF16)
        return rows(
            [
                lanes([turned[x - o + 1, dy] if abs(x - o) <= 1 else blank for o in outs])
                for dy in range(3)
                for x in xs
            ]
        )

    def finish_middle(i, j, part):
        middle[i, j] = leaky(part + b2[...]).astype(BF16)

    def finish_final(i, j, part):
        grown = coarse[2 + i, 2 + j].astype(F32) + leaky(part + b3[...])
        final[1 + i, 1 + j] = grown.astype(BF16)

    def meanwhile():
        start(SKIP, CORNERS)
        start(SKIP, FACES_X)
        start(SKIP, FACES_Y)
        loaded(w3, b3)
        turn_weights(w3, turned3)
        loaded(w4, b4, bu)
        arrange(w4, big4, edge4)
        column(1, bu)
        column(2, b4)

    arrived(COARSE, FACES_Y)
    high = CY + 2
    made = nn(taken(coarse, (2, 3), high), weights(turned2, (2, 3), (2, 3)))
    mine[1] = made[:, : 3 * C2]
    mine[2] = made[:, 3 * C2 :]
    mine[0] = nn(taken(coarse, (2,), high), weights(turned2, (2,), (1,)))
    mine[3] = nn(taken(coarse, (3,), high), weights(turned2, (3,), (4,)))
    meanwhile()

    def ring_side(side, first):
        far, near, outs = (0, 1, (1, 2)) if side == 0 else (5, 4, (3, 4))
        arrived(COARSE, ways_of(1 - 2 * side), (side,))
        o = outs[side]
        mine[o - 1] = mine[o - 1] + nn(taken(coarse, (far,), high), weights(turned2, (far,), (o,)))
        arrived(COARSE, ways_of(1 - 2 * side), (1 - side,))
        made = nn(taken(coarse, (near,), high), weights(turned2, (near,), outs))
        for k, o in enumerate(outs):
            total = mine[o - 1] + made[:, 3 * C2 * k : 3 * C2 * (k + 1)]
            for j in range(high):
                finish_middle(o - 1, j, along_z(total[j * HALF : (j + 1) * HALF]))
        if first:
            xs = (2 * side, 2 * side + 1)
            third[...] = nn(taken(middle, xs, CY), weights(turned3, xs, (1, 2)))
            return
        for i in (side, 1 - side):
            xs = (2 * side, 2 * side + 1) if i == side else (1 + side,)
            made = nn(taken(middle, xs, CY), weights(turned3, xs, (1 + i,)))
            total = third[:, pl.ds(3 * C2 * i, 3 * C2)] + made
            for j in range(CY):
                finish_final(i, j, along_z(total[j * HALF : (j + 1) * HALF]))
            start(FINAL, ways_of(2 * i - 1))

    each_side(ring_side)
    start(FINAL, FACES_Y)

    loaded(wu)
    at_row = lax.broadcasted_iota(jnp.int32, (2 * HALF, 4 * NZ), 0)
    at_lane = lax.broadcasted_iota(jnp.int32, (2 * HALF, 4 * NZ), 1)
    place = (
        (at_row // HALF == lax.rem(at_lane, 2 * NZ) // NZ)
        & (lax.rem(at_lane, NZ) == 2 * lax.rem(at_row, HALF) + at_lane // (2 * NZ))
    ).astype(F32).astype(BF16)

    def lift(cells, parts):
        wide = []
        for k in range(0, len(cells), 2):
            two = rows([final[i, j] for i, j in cells[k : k + 2]]).T
            spread = nn(two, place).astype(BF16)
            wide.append(rows([spread[:, : 2 * NZ], spread[:, 2 * NZ :]]))
        made = nn(rows([lanes([wu[px, py, 0], wu[px, py, 1]]) for px, py, _ in parts]), lanes(wide))
        for k, (_, _, places) in enumerate(parts):
            for t, spot in enumerate(places):
                if spot is None:
                    continue
                x, y = spot
                value = leaky(made[C1 * k : C1 * (k + 1), NZ * t : NZ * (t + 1)] + col[1])
                merged[x, y] = (value + skip[x, y].astype(F32)).astype(BF16)

    def lift_all(cells, which):
        parts = []
        for px, py in which:
            places = [(2 * i - 1 + px, 2 * j - 1 + py) for i, j in cells]
            parts.append((px, py, [(x, y) if 0 <= y < FY + 2 else None for x, y in places]))
        lift(cells, parts)

    every = [(px, py) for px in range(2) for py in range(2)]
    for i in range(1, 1 + CX):
        lift_all([(i, j) for j in range(1, 1 + CY)], every)
    conv_own(merged, big4, (2, 3, 4, 5), finish_last)
    arrived(SKIP, FACES_Y)
    arrived(FINAL, FACES_Y)
    lift_all([(1, 0), (2, 0)], [(0, 1), (1, 1)])
    lift_all([(1, CY + 1), (2, CY + 1)], [(0, 0), (1, 0)])
    conv_own(merged, big4, (0, 1, 6, 7), finish_last)
    for phase in (IN, COARSE, SKIP):
        sent(phase)
    for side in (1, 0):
        arrived(SKIP, ways_of(1 - 2 * side))
        arrived(FINAL, ways_of(1 - 2 * side))
        i, px = ((0, 1), (CX + 1, 0))[side]
        lift_all([(i, j) for j in range(CY + 2)], [(px, 0), (px, 1)])
        conv_edge(merged, edge4, side, range(FY), finish_last)
    out[...] = flat[...].astype(BF16)
    sent(FINAL)


def body(nx, ny, x, w1, b1, wd, bd, w2, b2, w3, b3, wu, bu, w4, b4):
    count = C1 * FX * FY
    any_space = pl.BlockSpec(memory_space=pl.ANY)
    padded = pltpu.VMEM((FX + 2, FY + 2, C1, NZ), BF16)
    padded_coarse = pltpu.VMEM((CX + 2, CY + 2, HALF, C2), BF16)
    conv = pltpu.VMEM((3, 3, 3, C1, C1), BF16)
    conv_coarse = pltpu.VMEM((3, 3, 3 * C2, C2), BF16)
    turned = pltpu.VMEM((3, 3, C2, 3 * C2), BF16)
    big = pltpu.VMEM((3 * FX * C1, 3 * FX * C1), BF16)
    edge = pltpu.VMEM((2, 3 * C1, 3 * C1), BF16)
    args = (
        x,
        w1,
        jnp.swapaxes(wd, 3, 4),
        w2.reshape(3, 3, 3 * C2, C2),
        w3.reshape(3, 3, 3 * C2, C2),
        wu,
        w4,
        b1.reshape(1, C1),
        bd.reshape(1, C2),
        b2.reshape(1, C2),
        b3.reshape(1, C2),
        bu.reshape(1, C1),
        b4.reshape(1, C1),
    )
    out = pl.pallas_call(
        functools.partial(kernel, nx, ny),
        out_shape=jax.ShapeDtypeStruct((count, NZ), BF16),
        in_specs=[any_space] * 13,
        out_specs=pl.BlockSpec(memory_space=pltpu.VMEM),
        scratch_shapes=[
            pltpu.VMEM((C1, FX, FY, NZ), BF16),
            pltpu.VMEM((2, C1, FY, NZ), BF16),
            pltpu.VMEM((count, NZ), F32),
            pltpu.VMEM((2, C1 * FY, NZ), F32),
            pltpu.VMEM((FY, 2, C1, NZ), F32),
            padded,
            padded,
            padded,
            pltpu.VMEM((CX + 4, CY + 4, HALF, C2), BF16),
            padded_coarse,
            padded_coarse,
            conv,
            conv,
            pltpu.VMEM((2, 2, 2, C1, C2), BF16),
            conv_coarse,
            conv_coarse,
            pltpu.VMEM((2, 2, 2, C1, C2), BF16),
            big,
            big,
            edge,
            edge,
            pltpu.VMEM((1, C1), F32),
            pltpu.VMEM((1, C2), F32),
            pltpu.VMEM((1, C2), F32),
            pltpu.VMEM((1, C2), F32),
            pltpu.VMEM((1, C1), F32),
            pltpu.VMEM((1, C1), F32),
            pltpu.VMEM((3, C1, NZ), F32),
            turned,
            turned,
            pltpu.VMEM((CX + 2, (CY + 2) * HALF, 3 * C2), F32),
            pltpu.VMEM((CY * HALF, CX * 3 * C2), F32),
            pltpu.SemaphoreType.DMA((4, 16)),
            pltpu.SemaphoreType.DMA((4, 16)),
            pltpu.SemaphoreType.DMA((13,)),
        ],
        compiler_params=pltpu.CompilerParams(
            collective_id=0, has_side_effects=True, vmem_limit_bytes=48 * 1024 * 1024
        ),
    )(*(pltpu.with_memory_space_constraint(arg, pltpu.HBM) for arg in args))
    return out.reshape(C1, FX, FY, NZ)


def solution(mesh):
    sharded = P(None, "gx", "gy", None)
    return jax.shard_map(
        functools.partial(body, mesh.shape["gx"], mesh.shape["gy"]),
        mesh=mesh,
        in_specs=(sharded,) + (P(),) * 12,
        out_specs=sharded,
        check_vma=False,
    )
```

```python
import functools

import jax
import jax.numpy as jnp
from jax import lax
from jax.experimental import pallas as pl
from jax.experimental.pallas import tpu as pltpu
from jax.sharding import PartitionSpec as P

BF16 = jnp.bfloat16
F32 = jnp.float32
MESH = pl.DeviceIdType.MESH

C1 = 64
C2 = 128
NZ = 128
HALF = NZ // 2
FX, FY = 4, 8
CX, CY = 2, 4
WAYS = ((1, 0), (-1, 0), (0, 1), (0, -1), (1, 1), (1, -1), (-1, 1), (-1, -1))
FACES_X = ((1, 0), (-1, 0))
FACES_Y = ((0, 1), (0, -1))
CORNERS = WAYS[4:]
IN, COARSE, SKIP, FINAL = range(4)


def leaky(values):
    return jnp.maximum(values, 0.2 * values)


def nn(a, b):
    return lax.dot_general(a, b, (((1,), (0,)), ((), ())), preferred_element_type=F32)


def nt(a, b):
    return lax.dot_general(a, b, (((1,), (1,)), ((), ())), preferred_element_type=F32)


def lanes(parts):
    return jnp.concatenate(parts, axis=1)


def rows(parts):
    return jnp.concatenate(parts, axis=0)


def span(step, size):
    return {1: (size, 0, 1), -1: (1, size + 1, 1), 0: (1, 1, size)}[step]


def kernel(
    nx,
    ny,
    x_hbm,
    w1_hbm,
    wd_hbm,
    w2_hbm,
    w3_hbm,
    wu_hbm,
    w4_hbm,
    b1_hbm,
    bd_hbm,
    b2_hbm,
    b3_hbm,
    bu_hbm,
    b4_hbm,
    out,
    xin,
    beside,
    flat,
    beside_flat,
    acc,
    fine,
    skip,
    merged,
    coarse,
    middle,
    final,
    w1,
    w4,
    wd,
    w2,
    w3,
    wu,
    big1,
    big4,
    edge1,
    edge4,
    b1,
    bd,
    b2,
    b3,
    bu,
    b4,
    col,
    turned2,
    turned3,
    mine,
    third,
    send_sem,
    recv_sem,
    load_sem,
):
    gx, gy = lax.axis_index("gx"), lax.axis_index("gy")

    def device(way):
        return (lax.rem(gx + way[0] + nx, nx), lax.rem(gy + way[1] + ny, ny))

    late_front = lax.rem(gx, nx // 2) == 0

    def each_side(body):
        for late, order in ((True, (1, 0)), (False, (0, 1))):

            @pl.when(late_front if late else jnp.logical_not(late_front))
            def _():
                for k, side in enumerate(order):
                    body(side, k == 0)

    barrier = pltpu.get_barrier_semaphore()
    for way in WAYS:
        pl.semaphore_signal(barrier, inc=1, device_id=device(way), device_id_type=MESH)

    pairs = (
        (x_hbm, xin),
        (w1_hbm, w1),
        (b1_hbm, b1),
        (w4_hbm, w4),
        (wd_hbm, wd),
        (bd_hbm, bd),
        (w2_hbm, w2),
        (b2_hbm, b2),
        (w3_hbm, w3),
        (b3_hbm, b3),
        (wu_hbm, wu),
        (bu_hbm, bu),
        (b4_hbm, b4),
    )
    loads = [pltpu.make_async_copy(s, d, load_sem.at[k]) for k, (s, d) in enumerate(pairs)]
    for load in loads:
        load.start()
    def loaded(*refs):
        for load, (_, ref) in zip(loads, pairs):
            if any(ref is r for r in refs):
                load.wait()

    loaded(xin)
    columns = [(x, y) for x in range(FX) for y in range(FY)]
    columns.sort(key=lambda pair: pair[1] not in (0, FY - 1))

    def turn_input(some):
        for x, y in some:
            tile = flat[pl.ds(x * FY + y, C1, stride=FX * FY), :]
            fine[1 + x, 1 + y] = tile.astype(BF16)

    flat[...] = xin[...].astype(F32).reshape(C1 * FX * FY, NZ)
    turn_input(columns[: 2 * FX])
    pl.semaphore_wait(barrier, len(WAYS))

    face_moves = [
        pltpu.make_async_remote_copy(
            src_ref=xin.at[:, (FX - 1) * (1 - side)],
            dst_ref=beside.at[side],
            send_sem=send_sem.at[IN, side],
            recv_sem=recv_sem.at[IN, side],
            device_id=device(FACES_X[side]),
            device_id_type=MESH,
        )
        for side in range(2)
    ]
    for move in face_moves:
        move.start()

    def piece(buffer, phase, slot, way, xs, ys):
        return pltpu.make_async_remote_copy(
            src_ref=buffer.at[pl.ds(xs[0], xs[2]), pl.ds(ys[0], ys[2])],
            dst_ref=buffer.at[pl.ds(xs[1], xs[2]), pl.ds(ys[1], ys[2])],
            send_sem=send_sem.at[phase, slot],
            recv_sem=recv_sem.at[phase, slot],
            device_id=device(way),
            device_id_type=MESH,
        )

    def copies(buffer, phase, wide, high, chunks):
        made = {}
        for k, way in enumerate(WAYS):
            xs, ys = span(way[0], wide), span(way[1], high)
            if way in FACES_X:
                made[way] = [
                    piece(buffer, phase, 8 + 4 * k + c, way, xs, (1 + first, 1 + first, count))
                    for c, (first, count) in enumerate(chunks)
                ]
            else:
                made[way] = [piece(buffer, phase, k, way, xs, ys)]
        return made

    moves = {
        SKIP: copies(skip, SKIP, FX, FY, [(0, FY // 2), (FY // 2, FY // 2)]),
        FINAL: copies(final, FINAL, CX, CY, [(0, CY)]),
    }
    column_x = {1: 0, -1: CX + 2, 0: 2}
    double_y = {1: (CY, 0, 2), -1: (2, CY + 2, 2), 0: (2, 2, CY)}
    moves[COARSE] = {
        way: [
            piece(coarse, COARSE, 2 * k + i, way, (2 + i, column_x[way[0]] + i, 1), double_y[way[1]])
            for i in range(CX)
        ]
        for k, way in enumerate(WAYS)
    }
    moves[IN] = {
        way: [piece(fine, IN, k, way, span(way[0], FX), span(way[1], FY))]
        for k, way in enumerate(WAYS)
        if k >= 2
    }
    for side in range(2):
        moves[IN][FACES_X[side]] = [face_moves[side]]

    def start(phase, ways=WAYS, chunks=None):
        for way in ways:
            for k, move in enumerate(moves[phase][way]):
                if chunks is None or k in chunks:
                    move.start()

    def arrived(phase, ways, chunks=None):
        for way in ways:
            for k, move in enumerate(moves[phase][way]):
                if chunks is None or k in chunks:
                    move.wait_recv()

    start(IN, CORNERS + FACES_Y)
    turn_input(columns[2 * FX :])

    def ways_of(step):
        return [(step, 1), (step, -1), (step, 0)]

    def column(slot, bias):
        square = (C1, C1)
        mask = lax.broadcasted_iota(jnp.int32, square, 0) == lax.broadcasted_iota(
            jnp.int32, square, 1
        )
        kept = jnp.where(mask, jnp.broadcast_to(bias[...], square), 0.0)
        col[slot] = jnp.broadcast_to(jnp.sum(kept, axis=1, keepdims=True), (C1, NZ))

    def arrange(w, big, edge):
        blank = jnp.zeros((C1, C1), BF16)
        for dz in range(3):
            for out_x in range(FX):
                row = (dz * FX + out_x) * C1
                for pair in range(FX * 3 // 2):
                    halves = []
                    for k in (2 * pair, 2 * pair + 1):
                        dx = k // 3 - out_x + 1
                        halves.append(w[dx, k % 3, dz] if 0 <= dx < 3 else blank)
                    big[pl.ds(row, C1), pl.ds(128 * pair, 128)] = lanes(halves)
            for side in range(2):
                row = pl.ds(dz * C1, C1)
                edge[side, row, pl.ds(0, 2 * C1)] = lanes([w[2 * side, 0, dz], w[2 * side, 1, dz]])
                edge[side, row, pl.ds(2 * C1, C1)] = w[2 * side, 2, dz]

    loaded(w1, b1)
    arrange(w1, big1, edge1)
    column(0, b1)

    def turn(part, count):
        return (
            pltpu.roll(part[:count], 1, 1)
            + part[count : 2 * count]
            + pltpu.roll(part[2 * count :], NZ - 1, 1)
        )

    def conv_own(field, big, ys, finish):
        window = [field[pl.ds(1, FX), pl.ds(y, 3)].reshape(FX * 3 * C1, NZ) for y in ys]
        made = nn(big[...], lanes(window))
        for t, y in enumerate(ys):
            total = turn(made[:, NZ * t : NZ * t + NZ], FX * C1)
            for x in range(FX):
                part = total[C1 * x : C1 * (x + 1)]
                if x in (0, FX - 1):
                    acc[y, x // (FX - 1)] = part
                else:
                    finish(x, y, part)

    def conv_edge(field, edge, side, ys, finish):
        window = [field[(FX + 1) * side, pl.ds(y, 3)].reshape(3 * C1, NZ) for y in ys]
        made = nn(edge[side], lanes(window))
        for t, y in enumerate(ys):
            part = acc[y, side] + turn(made[:, NZ * t : NZ * t + NZ], C1)
            finish((FX - 1) * side, y, part)

    def finish_first(x, y, part):
        skip[1 + x, 1 + y] = leaky(part + col[0]).astype(BF16)

    def finish_last(x, y, part):
        flat[pl.ds(x * FY + y, C1, stride=FX * FY), :] = part + col[2]

    def turn_weights(w, turned):
        for dx in range(3):
            for dy in range(3):
                turned[dx, dy] = w[dx, dy].T

    conv_own(fine, big1, (2, 3, 4, 5), finish_first)
    arrived(IN, FACES_Y)
    conv_own(fine, big1, (0, 1, 6, 7), finish_first)

    loaded(wd, bd)
    at_row = lax.broadcasted_iota(jnp.int32, (NZ, NZ), 0)
    at_lane = lax.broadcasted_iota(jnp.int32, (NZ, NZ), 1)
    pick = (at_lane == 2 * lax.rem(at_row, HALF) + at_row // HALF).astype(F32).astype(BF16)
    down = rows([wd[px, py, pz] for pz in range(2) for px in range(2) for py in range(2)])
    def take_side(side, _):
        for move in moves[IN][FACES_X[side]]:
            move.wait_recv()
        beside_flat[side] = beside[side].astype(F32).reshape(C1 * FY, NZ)
        for y in range(FY):
            tile = beside_flat[side, pl.ds(y, C1, stride=FY), :]
            fine[(FX + 1) * side, 1 + y] = tile.astype(BF16)
        arrived(IN, ways_of(1 - 2 * side)[:2])
        conv_edge(fine, edge1, side, range(FY), finish_first)

        split = []
        for j in range(CY):
            block = skip[pl.ds(1 + 2 * side, 2), pl.ds(1 + 2 * j, 2)].reshape(4 * C1, NZ)
            moved = nt(pick, block).astype(BF16)
            split.append(lanes([moved[:HALF], moved[HALF:]]))
        value = leaky(nn(rows(split), down) + bd[...]).astype(BF16)
        coarse[2 + side, pl.ds(2, CY)] = value.reshape(CY, HALF, C2)
        start(COARSE, ways_of(2 * side - 1) + ways_of(1 - 2 * side), (side,))
        start(COARSE, FACES_Y, (side,))

    loaded(w2, b2)
    turn_weights(w2, turned2)
    each_side(take_side)

    def sent(phase):
        for way in WAYS:
            for move in moves[phase][way]:
                move.wait_send()

    def along_z(part):
        return (
            pltpu.roll(part[:, :C2], 1, 0)
            + part[:, C2 : 2 * C2]
            + pltpu.roll(part[:, 2 * C2 :], HALF - 1, 0)
        )

    def taken(field, xs, high):
        return lanes(
            [field[x, pl.ds(dy, high)].reshape(high * HALF, C2) for dy in range(3) for x in xs]
        )

    def weights(turned, xs, outs):
        blank = jnp.zeros((C2, 3 * C2), BF16)
        return rows(
            [
                lanes([turned[x - o + 1, dy] if abs(x - o) <= 1 else blank for o in outs])
                for dy in range(3)
                for x in xs
            ]
        )

    def finish_middle(i, j, part):
        middle[i, j] = leaky(part + b2[...]).astype(BF16)

    def finish_final(i, j, part):
        grown = coarse[2 + i, 2 + j].astype(F32) + leaky(part + b3[...])
        final[1 + i, 1 + j] = grown.astype(BF16)

    loaded(w3, b3)
    turn_weights(w3, turned3)
    loaded(w4, b4, bu)
    arrange(w4, big4, edge4)
    column(1, bu)
    column(2, b4)

    arrived(COARSE, FACES_Y)
    high = CY + 2
    made = nn(taken(coarse, (2, 3), high), weights(turned2, (2, 3), (2, 3)))
    mine[1] = made[:, : 3 * C2]
    mine[2] = made[:, 3 * C2 :]
    mine[0] = nn(taken(coarse, (2,), high), weights(turned2, (2,), (1,)))
    mine[3] = nn(taken(coarse, (3,), high), weights(turned2, (3,), (4,)))
    start(SKIP, CORNERS)
    start(SKIP, FACES_X)
    start(SKIP, FACES_Y)

    def ring_side(side, first):
        far, near, outs = (0, 1, (1, 2)) if side == 0 else (5, 4, (3, 4))
        arrived(COARSE, ways_of(1 - 2 * side), (side,))
        o = outs[side]
        mine[o - 1] = mine[o - 1] + nn(taken(coarse, (far,), high), weights(turned2, (far,), (o,)))
        arrived(COARSE, ways_of(1 - 2 * side), (1 - side,))
        made = nn(taken(coarse, (near,), high), weights(turned2, (near,), outs))
        for k, o in enumerate(outs):
            total = mine[o - 1] + made[:, 3 * C2 * k : 3 * C2 * (k + 1)]
            for j in range(high):
                finish_middle(o - 1, j, along_z(total[j * HALF : (j + 1) * HALF]))
        if first:
            xs = (2 * side, 2 * side + 1)
            third[...] = nn(taken(middle, xs, CY), weights(turned3, xs, (1, 2)))
            return
        for i in (side, 1 - side):
            xs = (2 * side, 2 * side + 1) if i == side else (1 + side,)
            made = nn(taken(middle, xs, CY), weights(turned3, xs, (1 + i,)))
            total = third[:, pl.ds(3 * C2 * i, 3 * C2)] + made
            for j in range(CY):
                finish_final(i, j, along_z(total[j * HALF : (j + 1) * HALF]))
            start(FINAL, ways_of(2 * i - 1))

    each_side(ring_side)
    start(FINAL, FACES_Y)

    loaded(wu)
    at_row = lax.broadcasted_iota(jnp.int32, (2 * HALF, 4 * NZ), 0)
    at_lane = lax.broadcasted_iota(jnp.int32, (2 * HALF, 4 * NZ), 1)
    place = (
        (at_row // HALF == lax.rem(at_lane, 2 * NZ) // NZ)
        & (lax.rem(at_lane, NZ) == 2 * lax.rem(at_row, HALF) + at_lane // (2 * NZ))
    ).astype(F32).astype(BF16)

    def lift(cells, parts):
        wide = []
        for k in range(0, len(cells), 2):
            two = rows([final[i, j] for i, j in cells[k : k + 2]]).T
            spread = nn(two, place).astype(BF16)
            wide.append(rows([spread[:, : 2 * NZ], spread[:, 2 * NZ :]]))
        made = nn(rows([lanes([wu[px, py, 0], wu[px, py, 1]]) for px, py, _ in parts]), lanes(wide))
        for k, (_, _, places) in enumerate(parts):
            for t, spot in enumerate(places):
                if spot is None:
                    continue
                x, y = spot
                value = leaky(made[C1 * k : C1 * (k + 1), NZ * t : NZ * (t + 1)] + col[1])
                merged[x, y] = (value + skip[x, y].astype(F32)).astype(BF16)

    def lift_all(cells, which):
        parts = []
        for px, py in which:
            places = [(2 * i - 1 + px, 2 * j - 1 + py) for i, j in cells]
            parts.append((px, py, [(x, y) if 0 <= y < FY + 2 else None for x, y in places]))
        lift(cells, parts)

    every = [(px, py) for px in range(2) for py in range(2)]
    for i in range(1, 1 + CX):
        lift_all([(i, j) for j in range(1, 1 + CY)], every)
    conv_own(merged, big4, (2, 3, 4, 5), finish_last)
    arrived(SKIP, FACES_Y)
    arrived(FINAL, FACES_Y)
    lift_all([(1, 0), (2, 0)], [(0, 1), (1, 1)])
    lift_all([(1, CY + 1), (2, CY + 1)], [(0, 0), (1, 0)])
    conv_own(merged, big4, (0, 1, 6, 7), finish_last)
    for phase in (IN, COARSE, SKIP):
        sent(phase)
    for side in (1, 0):
        arrived(SKIP, ways_of(1 - 2 * side))
        arrived(FINAL, ways_of(1 - 2 * side))
        i, px = ((0, 1), (CX + 1, 0))[side]
        lift_all([(i, j) for j in range(CY + 2)], [(px, 0), (px, 1)])
        conv_edge(merged, edge4, side, range(FY), finish_last)
    out[...] = flat[...].astype(BF16)
    sent(FINAL)


def body(nx, ny, x, w1, b1, wd, bd, w2, b2, w3, b3, wu, bu, w4, b4):
    count = C1 * FX * FY
    any_space = pl.BlockSpec(memory_space=pl.ANY)
    padded = pltpu.VMEM((FX + 2, FY + 2, C1, NZ), BF16)
    padded_coarse = pltpu.VMEM((CX + 2, CY + 2, HALF, C2), BF16)
    conv = pltpu.VMEM((3, 3, 3, C1, C1), BF16)
    conv_coarse = pltpu.VMEM((3, 3, 3 * C2, C2), BF16)
    turned = pltpu.VMEM((3, 3, C2, 3 * C2), BF16)
    big = pltpu.VMEM((3 * FX * C1, 3 * FX * C1), BF16)
    edge = pltpu.VMEM((2, 3 * C1, 3 * C1), BF16)
    args = (
        x,
        w1,
        jnp.swapaxes(wd, 3, 4),
        w2.reshape(3, 3, 3 * C2, C2),
        w3.reshape(3, 3, 3 * C2, C2),
        wu,
        w4,
        b1.reshape(1, C1),
        bd.reshape(1, C2),
        b2.reshape(1, C2),
        b3.reshape(1, C2),
        bu.reshape(1, C1),
        b4.reshape(1, C1),
    )
    out = pl.pallas_call(
        functools.partial(kernel, nx, ny),
        out_shape=jax.ShapeDtypeStruct((count, NZ), BF16),
        in_specs=[any_space] * 13,
        out_specs=pl.BlockSpec(memory_space=pltpu.VMEM),
        scratch_shapes=[
            pltpu.VMEM((C1, FX, FY, NZ), BF16),
            pltpu.VMEM((2, C1, FY, NZ), BF16),
            pltpu.VMEM((count, NZ), F32),
            pltpu.VMEM((2, C1 * FY, NZ), F32),
            pltpu.VMEM((FY, 2, C1, NZ), F32),
            padded,
            padded,
            padded,
            pltpu.VMEM((CX + 4, CY + 4, HALF, C2), BF16),
            padded_coarse,
            padded_coarse,
            conv,
            conv,
            pltpu.VMEM((2, 2, 2, C1, C2), BF16),
            conv_coarse,
            conv_coarse,
            pltpu.VMEM((2, 2, 2, C1, C2), BF16),
            big,
            big,
            edge,
            edge,
            pltpu.VMEM((1, C1), F32),
            pltpu.VMEM((1, C2), F32),
            pltpu.VMEM((1, C2), F32),
            pltpu.VMEM((1, C2), F32),
            pltpu.VMEM((1, C1), F32),
            pltpu.VMEM((1, C1), F32),
            pltpu.VMEM((3, C1, NZ), F32),
            turned,
            turned,
            pltpu.VMEM((CX + 2, (CY + 2) * HALF, 3 * C2), F32),
            pltpu.VMEM((CY * HALF, CX * 3 * C2), F32),
            pltpu.SemaphoreType.DMA((4, 16)),
            pltpu.SemaphoreType.DMA((4, 16)),
            pltpu.SemaphoreType.DMA((13,)),
        ],
        compiler_params=pltpu.CompilerParams(
            collective_id=0, has_side_effects=True, vmem_limit_bytes=48 * 1024 * 1024
        ),
    )(*(pltpu.with_memory_space_constraint(arg, pltpu.HBM) for arg in args))
    return out.reshape(C1, FX, FY, NZ)


def solution(mesh):
    sharded = P(None, "gx", "gy", None)
    return jax.shard_map(
        functools.partial(body, mesh.shape["gx"], mesh.shape["gy"]),
        mesh=mesh,
        in_specs=(sharded,) + (P(),) * 12,
        out_specs=sharded,
        check_vma=False,
    )
```

```python
import functools

import jax
import jax.numpy as jnp
from jax import lax
from jax.experimental import pallas as pl
from jax.experimental.pallas import tpu as pltpu
from jax.sharding import PartitionSpec as P

BF16 = jnp.bfloat16
F32 = jnp.float32
MESH = pl.DeviceIdType.MESH

C1 = 64
C2 = 128
NZ = 128
HALF = NZ // 2
FX, FY = 4, 8
CX, CY = 2, 4
WAYS = ((1, 0), (-1, 0), (0, 1), (0, -1), (1, 1), (1, -1), (-1, 1), (-1, -1))
FACES_X = ((1, 0), (-1, 0))
FACES_Y = ((0, 1), (0, -1))
CORNERS = WAYS[4:]
IN, COARSE, SKIP, FINAL = range(4)


def leaky(values):
    return jnp.maximum(values, 0.2 * values)


def nn(a, b):
    return lax.dot_general(a, b, (((1,), (0,)), ((), ())), preferred_element_type=F32)


def nt(a, b):
    return lax.dot_general(a, b, (((1,), (1,)), ((), ())), preferred_element_type=F32)


def lanes(parts):
    return jnp.concatenate(parts, axis=1)


def rows(parts):
    return jnp.concatenate(parts, axis=0)


def span(step, size):
    return {1: (size, 0, 1), -1: (1, size + 1, 1), 0: (1, 1, size)}[step]


def kernel(
    nx,
    ny,
    x_hbm,
    w1_hbm,
    wd_hbm,
    w2_hbm,
    w3_hbm,
    wu_hbm,
    w4_hbm,
    b1_hbm,
    bd_hbm,
    b2_hbm,
    b3_hbm,
    bu_hbm,
    b4_hbm,
    out,
    xin,
    beside,
    flat,
    beside_flat,
    acc,
    fine,
    skip,
    merged,
    coarse,
    middle,
    final,
    w1,
    w4,
    wd,
    w2,
    w3,
    wu,
    big1,
    big4,
    edge1,
    edge4,
    b1,
    bd,
    b2,
    b3,
    bu,
    b4,
    col,
    turned2,
    turned3,
    mine,
    third,
    send_sem,
    recv_sem,
    load_sem,
):
    gx, gy = lax.axis_index("gx"), lax.axis_index("gy")

    def device(way):
        return (lax.rem(gx + way[0] + nx, nx), lax.rem(gy + way[1] + ny, ny))

    late_front = lax.rem(gx, nx // 2) == 0

    def each_side(body):
        for late, order in ((True, (1, 0)), (False, (0, 1))):

            @pl.when(late_front if late else jnp.logical_not(late_front))
            def _():
                for k, side in enumerate(order):
                    body(side, k == 0)

    barrier = pltpu.get_barrier_semaphore()
    for way in WAYS:
        pl.semaphore_signal(barrier, inc=1, device_id=device(way), device_id_type=MESH)

    pairs = (
        (x_hbm, xin),
        (w1_hbm, w1),
        (b1_hbm, b1),
        (w4_hbm, w4),
        (wd_hbm, wd),
        (bd_hbm, bd),
        (w2_hbm, w2),
        (b2_hbm, b2),
        (w3_hbm, w3),
        (b3_hbm, b3),
        (wu_hbm, wu),
        (bu_hbm, bu),
        (b4_hbm, b4),
    )
    loads = [pltpu.make_async_copy(s, d, load_sem.at[k]) for k, (s, d) in enumerate(pairs)]
    for load in loads:
        load.start()
    def loaded(*refs):
        for load, (_, ref) in zip(loads, pairs):
            if any(ref is r for r in refs):
                load.wait()

    loaded(xin)
    pl.semaphore_wait(barrier, len(WAYS))

    face_moves = [
        pltpu.make_async_remote_copy(
            src_ref=xin.at[:, (FX - 1) * (1 - side)],
            dst_ref=beside.at[side],
            send_sem=send_sem.at[IN, side],
            recv_sem=recv_sem.at[IN, side],
            device_id=device(FACES_X[side]),
            device_id_type=MESH,
        )
        for side in range(2)
    ]
    for move in face_moves:
        move.start()

    def piece(buffer, phase, slot, way, xs, ys):
        return pltpu.make_async_remote_copy(
            src_ref=buffer.at[pl.ds(xs[0], xs[2]), pl.ds(ys[0], ys[2])],
            dst_ref=buffer.at[pl.ds(xs[1], xs[2]), pl.ds(ys[1], ys[2])],
            send_sem=send_sem.at[phase, slot],
            recv_sem=recv_sem.at[phase, slot],
            device_id=device(way),
            device_id_type=MESH,
        )

    def copies(buffer, phase, wide, high, chunks):
        made = {}
        for k, way in enumerate(WAYS):
            xs, ys = span(way[0], wide), span(way[1], high)
            if way in FACES_X:
                made[way] = [
                    piece(buffer, phase, 8 + 4 * k + c, way, xs, (1 + first, 1 + first, count))
                    for c, (first, count) in enumerate(chunks)
                ]
            else:
                made[way] = [piece(buffer, phase, k, way, xs, ys)]
        return made

    moves = {
        SKIP: copies(skip, SKIP, FX, FY, [(0, FY // 2), (FY // 2, FY // 2)]),
        FINAL: copies(final, FINAL, CX, CY, [(0, CY)]),
    }
    column_x = {1: 0, -1: CX + 2, 0: 2}
    double_y = {1: (CY, 0, 2), -1: (2, CY + 2, 2), 0: (2, 2, CY)}
    moves[COARSE] = {
        way: [
            piece(coarse, COARSE, 2 * k + i, way, (2 + i, column_x[way[0]] + i, 1), double_y[way[1]])
            for i in range(CX)
        ]
        for k, way in enumerate(WAYS)
    }
    moves[IN] = {
        way: [piece(fine, IN, k, way, span(way[0], FX), span(way[1], FY))]
        for k, way in enumerate(WAYS)
        if k >= 2
    }
    for side in range(2):
        moves[IN][FACES_X[side]] = [face_moves[side]]

    def start(phase, ways=WAYS, chunks=None):
        for way in ways:
            for k, move in enumerate(moves[phase][way]):
                if chunks is None or k in chunks:
                    move.start()

    def arrived(phase, ways, chunks=None):
        for way in ways:
            for k, move in enumerate(moves[phase][way]):
                if chunks is None or k in chunks:
                    move.wait_recv()

    flat[...] = xin[...].astype(F32).reshape(C1 * FX * FY, NZ)
    columns = [(x, y) for x in range(FX) for y in range(FY)]

    def end(pair):
        return (pair[1] in (0, FY - 1)) + (pair[1] in (0, FY - 1) and pair[0] in (0, FX - 1))

    columns.sort(key=end, reverse=True)
    for k, (x, y) in enumerate(columns):
        tile = flat[pl.ds(x * FY + y, C1, stride=FX * FY), :]
        fine[1 + x, 1 + y] = tile.astype(BF16)
        if k == len(CORNERS) - 1:
            start(IN, CORNERS)
        if k == 2 * FX - 1:
            start(IN, FACES_Y)

    def ways_of(step):
        return [(step, 1), (step, -1), (step, 0)]

    def column(slot, bias):
        square = (C1, C1)
        mask = lax.broadcasted_iota(jnp.int32, square, 0) == lax.broadcasted_iota(
            jnp.int32, square, 1
        )
        kept = jnp.where(mask, jnp.broadcast_to(bias[...], square), 0.0)
        col[slot] = jnp.broadcast_to(jnp.sum(kept, axis=1, keepdims=True), (C1, NZ))

    def arrange(w, big, edge):
        blank = jnp.zeros((C1, C1), BF16)
        for dz in range(3):
            for out_x in range(FX):
                row = (dz * FX + out_x) * C1
                for pair in range(FX * 3 // 2):
                    halves = []
                    for k in (2 * pair, 2 * pair + 1):
                        dx = k // 3 - out_x + 1
                        halves.append(w[dx, k % 3, dz] if 0 <= dx < 3 else blank)
                    big[pl.ds(row, C1), pl.ds(128 * pair, 128)] = lanes(halves)
            for side in range(2):
                row = pl.ds(dz * C1, C1)
                edge[side, row, pl.ds(0, 2 * C1)] = lanes([w[2 * side, 0, dz], w[2 * side, 1, dz]])
                edge[side, row, pl.ds(2 * C1, C1)] = w[2 * side, 2, dz]

    loaded(w1, b1)
    arrange(w1, big1, edge1)
    column(0, b1)

    def turn(part, count):
        return (
            pltpu.roll(part[:count], 1, 1)
            + part[count : 2 * count]
            + pltpu.roll(part[2 * count :], NZ - 1, 1)
        )

    def conv_own(field, big, ys, finish):
        window = [field[pl.ds(1, FX), pl.ds(y, 3)].reshape(FX * 3 * C1, NZ) for y in ys]
        made = nn(big[...], lanes(window))
        for t, y in enumerate(ys):
            total = turn(made[:, NZ * t : NZ * t + NZ], FX * C1)
            for x in range(FX):
                part = total[C1 * x : C1 * (x + 1)]
                if x in (0, FX - 1):
                    acc[y, x // (FX - 1)] = part
                else:
                    finish(x, y, part)

    def conv_edge(field, edge, side, ys, finish):
        window = [field[(FX + 1) * side, pl.ds(y, 3)].reshape(3 * C1, NZ) for y in ys]
        made = nn(edge[side], lanes(window))
        for t, y in enumerate(ys):
            part = acc[y, side] + turn(made[:, NZ * t : NZ * t + NZ], C1)
            finish((FX - 1) * side, y, part)

    def finish_first(x, y, part):
        skip[1 + x, 1 + y] = leaky(part + col[0]).astype(BF16)

    def finish_last(x, y, part):
        flat[pl.ds(x * FY + y, C1, stride=FX * FY), :] = part + col[2]

    def turn_weights(w, turned):
        for dx in range(3):
            for dy in range(3):
                turned[dx, dy] = w[dx, dy].T

    conv_own(fine, big1, (2, 3, 4, 5), finish_first)
    arrived(IN, FACES_Y)
    conv_own(fine, big1, (0, 1, 6, 7), finish_first)

    loaded(wd, bd)
    at_row = lax.broadcasted_iota(jnp.int32, (NZ, NZ), 0)
    at_lane = lax.broadcasted_iota(jnp.int32, (NZ, NZ), 1)
    pick = (at_lane == 2 * lax.rem(at_row, HALF) + at_row // HALF).astype(F32).astype(BF16)
    down = rows([wd[px, py, pz] for pz in range(2) for px in range(2) for py in range(2)])
    def take_side(side, _):
        for move in moves[IN][FACES_X[side]]:
            move.wait_recv()
        beside_flat[side] = beside[side].astype(F32).reshape(C1 * FY, NZ)
        for y in range(FY):
            tile = beside_flat[side, pl.ds(y, C1, stride=FY), :]
            fine[(FX + 1) * side, 1 + y] = tile.astype(BF16)
        arrived(IN, ways_of(1 - 2 * side)[:2])
        conv_edge(fine, edge1, side, range(FY), finish_first)

        split = []
        for j in range(CY):
            block = skip[pl.ds(1 + 2 * side, 2), pl.ds(1 + 2 * j, 2)].reshape(4 * C1, NZ)
            moved = nt(pick, block).astype(BF16)
            split.append(lanes([moved[:HALF], moved[HALF:]]))
        value = leaky(nn(rows(split), down) + bd[...]).astype(BF16)
        coarse[2 + side, pl.ds(2, CY)] = value.reshape(CY, HALF, C2)
        start(COARSE, CORNERS + FACES_X + FACES_Y, (side,))

    loaded(w2, b2)
    turn_weights(w2, turned2)
    each_side(take_side)

    def sent(phase):
        for way in WAYS:
            for move in moves[phase][way]:
                move.wait_send()

    def along_z(part):
        return (
            pltpu.roll(part[:, :C2], 1, 0)
            + part[:, C2 : 2 * C2]
            + pltpu.roll(part[:, 2 * C2 :], HALF - 1, 0)
        )

    def taken(field, xs, high):
        return lanes(
            [field[x, pl.ds(dy, high)].reshape(high * HALF, C2) for dy in range(3) for x in xs]
        )

    def weights(turned, xs, outs):
        blank = jnp.zeros((C2, 3 * C2), BF16)
        return rows(
            [
                lanes([turned[x - o + 1, dy] if abs(x - o) <= 1 else blank for o in outs])
                for dy in range(3)
                for x in xs
            ]
        )

    def finish_middle(i, j, part):
        middle[i, j] = leaky(part + b2[...]).astype(BF16)

    def finish_final(i, j, part):
        grown = coarse[2 + i, 2 + j].astype(F32) + leaky(part + b3[...])
        final[1 + i, 1 + j] = grown.astype(BF16)

    def meanwhile():
        start(SKIP, CORNERS)
        start(SKIP, FACES_X)
        start(SKIP, FACES_Y)
        loaded(w3, b3)
        turn_weights(w3, turned3)
        loaded(w4, b4, bu)
        arrange(w4, big4, edge4)
        column(1, bu)
        column(2, b4)

    arrived(COARSE, FACES_Y)
    high = CY + 2
    made = nn(taken(coarse, (2, 3), high), weights(turned2, (2, 3), (2, 3)))
    mine[1] = made[:, : 3 * C2]
    mine[2] = made[:, 3 * C2 :]
    mine[0] = nn(taken(coarse, (2,), high), weights(turned2, (2,), (1,)))
    mine[3] = nn(taken(coarse, (3,), high), weights(turned2, (3,), (4,)))
    meanwhile()

    def ring_side(side, first):
        far, near, outs = (0, 1, (1, 2)) if side == 0 else (5, 4, (3, 4))
        arrived(COARSE, ways_of(1 - 2 * side), (side,))
        o = outs[side]
        mine[o - 1] = mine[o - 1] + nn(taken(coarse, (far,), high), weights(turned2, (far,), (o,)))
        arrived(COARSE, ways_of(1 - 2 * side), (1 - side,))
        made = nn(taken(coarse, (near,), high), weights(turned2, (near,), outs))
        for k, o in enumerate(outs):
            total = mine[o - 1] + made[:, 3 * C2 * k : 3 * C2 * (k + 1)]
            for j in range(high):
                finish_middle(o - 1, j, along_z(total[j * HALF : (j + 1) * HALF]))
        if first:
            xs = (2 * side, 2 * side + 1)
            third[...] = nn(taken(middle, xs, CY), weights(turned3, xs, (1, 2)))
            return
        for i in (side, 1 - side):
            xs = (2 * side, 2 * side + 1) if i == side else (1 + side,)
            made = nn(taken(middle, xs, CY), weights(turned3, xs, (1 + i,)))
            total = third[:, pl.ds(3 * C2 * i, 3 * C2)] + made
            for j in range(CY):
                finish_final(i, j, along_z(total[j * HALF : (j + 1) * HALF]))
            start(FINAL, ways_of(2 * i - 1))

    each_side(ring_side)
    start(FINAL, FACES_Y)

    loaded(wu)
    at_row = lax.broadcasted_iota(jnp.int32, (2 * HALF, 4 * NZ), 0)
    at_lane = lax.broadcasted_iota(jnp.int32, (2 * HALF, 4 * NZ), 1)
    place = (
        (at_row // HALF == lax.rem(at_lane, 2 * NZ) // NZ)
        & (lax.rem(at_lane, NZ) == 2 * lax.rem(at_row, HALF) + at_lane // (2 * NZ))
    ).astype(F32).astype(BF16)

    def lift(cells, parts):
        wide = []
        for k in range(0, len(cells), 2):
            two = rows([final[i, j] for i, j in cells[k : k + 2]]).T
            spread = nn(two, place).astype(BF16)
            wide.append(rows([spread[:, : 2 * NZ], spread[:, 2 * NZ :]]))
        made = nn(rows([lanes([wu[px, py, 0], wu[px, py, 1]]) for px, py, _ in parts]), lanes(wide))
        for k, (_, _, places) in enumerate(parts):
            for t, spot in enumerate(places):
                if spot is None:
                    continue
                x, y = spot
                value = leaky(made[C1 * k : C1 * (k + 1), NZ * t : NZ * (t + 1)] + col[1])
                merged[x, y] = (value + skip[x, y].astype(F32)).astype(BF16)

    def lift_all(cells, which):
        parts = []
        for px, py in which:
            places = [(2 * i - 1 + px, 2 * j - 1 + py) for i, j in cells]
            parts.append((px, py, [(x, y) if 0 <= y < FY + 2 else None for x, y in places]))
        lift(cells, parts)

    every = [(px, py) for px in range(2) for py in range(2)]
    for i in range(1, 1 + CX):
        lift_all([(i, j) for j in range(1, 1 + CY)], every)
    conv_own(merged, big4, (2, 3, 4, 5), finish_last)
    arrived(SKIP, FACES_Y)
    arrived(FINAL, FACES_Y)
    lift_all([(1, 0), (2, 0)], [(0, 1), (1, 1)])
    lift_all([(1, CY + 1), (2, CY + 1)], [(0, 0), (1, 0)])
    conv_own(merged, big4, (0, 1, 6, 7), finish_last)
    for phase in (IN, COARSE, SKIP):
        sent(phase)
    for side in (1, 0):
        arrived(SKIP, ways_of(1 - 2 * side))
        arrived(FINAL, ways_of(1 - 2 * side))
        i, px = ((0, 1), (CX + 1, 0))[side]
        lift_all([(i, j) for j in range(CY + 2)], [(px, 0), (px, 1)])
        conv_edge(merged, edge4, side, range(FY), finish_last)
    out[...] = flat[...].astype(BF16)
    sent(FINAL)


def body(nx, ny, x, w1, b1, wd, bd, w2, b2, w3, b3, wu, bu, w4, b4):
    count = C1 * FX * FY
    any_space = pl.BlockSpec(memory_space=pl.ANY)
    padded = pltpu.VMEM((FX + 2, FY + 2, C1, NZ), BF16)
    padded_coarse = pltpu.VMEM((CX + 2, CY + 2, HALF, C2), BF16)
    conv = pltpu.VMEM((3, 3, 3, C1, C1), BF16)
    conv_coarse = pltpu.VMEM((3, 3, 3 * C2, C2), BF16)
    turned = pltpu.VMEM((3, 3, C2, 3 * C2), BF16)
    big = pltpu.VMEM((3 * FX * C1, 3 * FX * C1), BF16)
    edge = pltpu.VMEM((2, 3 * C1, 3 * C1), BF16)
    args = (
        x,
        w1,
        jnp.swapaxes(wd, 3, 4),
        w2.reshape(3, 3, 3 * C2, C2),
        w3.reshape(3, 3, 3 * C2, C2),
        wu,
        w4,
        b1.reshape(1, C1),
        bd.reshape(1, C2),
        b2.reshape(1, C2),
        b3.reshape(1, C2),
        bu.reshape(1, C1),
        b4.reshape(1, C1),
    )
    out = pl.pallas_call(
        functools.partial(kernel, nx, ny),
        out_shape=jax.ShapeDtypeStruct((count, NZ), BF16),
        in_specs=[any_space] * 13,
        out_specs=pl.BlockSpec(memory_space=pltpu.VMEM),
        scratch_shapes=[
            pltpu.VMEM((C1, FX, FY, NZ), BF16),
            pltpu.VMEM((2, C1, FY, NZ), BF16),
            pltpu.VMEM((count, NZ), F32),
            pltpu.VMEM((2, C1 * FY, NZ), F32),
            pltpu.VMEM((FY, 2, C1, NZ), F32),
            padded,
            padded,
            padded,
            pltpu.VMEM((CX + 4, CY + 4, HALF, C2), BF16),
            padded_coarse,
            padded_coarse,
            conv,
            conv,
            pltpu.VMEM((2, 2, 2, C1, C2), BF16),
            conv_coarse,
            conv_coarse,
            pltpu.VMEM((2, 2, 2, C1, C2), BF16),
            big,
            big,
            edge,
            edge,
            pltpu.VMEM((1, C1), F32),
            pltpu.VMEM((1, C2), F32),
            pltpu.VMEM((1, C2), F32),
            pltpu.VMEM((1, C2), F32),
            pltpu.VMEM((1, C1), F32),
            pltpu.VMEM((1, C1), F32),
            pltpu.VMEM((3, C1, NZ), F32),
            turned,
            turned,
            pltpu.VMEM((CX + 2, (CY + 2) * HALF, 3 * C2), F32),
            pltpu.VMEM((CY * HALF, CX * 3 * C2), F32),
            pltpu.SemaphoreType.DMA((4, 16)),
            pltpu.SemaphoreType.DMA((4, 16)),
            pltpu.SemaphoreType.DMA((13,)),
        ],
        compiler_params=pltpu.CompilerParams(
            collective_id=0, has_side_effects=True, vmem_limit_bytes=48 * 1024 * 1024
        ),
    )(*(pltpu.with_memory_space_constraint(arg, pltpu.HBM) for arg in args))
    return out.reshape(C1, FX, FY, NZ)


def solution(mesh):
    sharded = P(None, "gx", "gy", None)
    return jax.shard_map(
        functools.partial(body, mesh.shape["gx"], mesh.shape["gy"]),
        mesh=mesh,
        in_specs=(sharded,) + (P(),) * 12,
        out_specs=sharded,
        check_vma=False,
    )
```
